128 devices in a mesh: blk: 16 (over y, z_hi, core), fsdp: 8 (over z_lo, x).
Axes of the slice: x: 4, y: 4, z: 4 (z_hi: 2, z_lo: 2; z = z_hi * 2 + z_lo), core: 2. Of those that a mesh axis runs over, the one named last changes fastest.
Arguments:
- x_forward: bfloat16 [32768, 4096], P(('blk', 'fsdp'))
- seg_forward: int32 [128, 256], P(('blk', 'fsdp')), may hold values from 0 to 3, never falling along the last dimension, each value on 1 to 128 neighbouring positions
- x_saved: bfloat16 [32768, 4096], P(('blk', 'fsdp'))
- x_earlier: bfloat16 [32768, 4096], P(('blk', 'fsdp'))
- cotangent: bfloat16 [32768, 4096], P(('blk', 'fsdp')), may hold values from -0.119628906 to 0.119628906
- seg_backward: int32 [128, 256], P(('blk', 'fsdp')), may hold values from 0 to 3, never falling along the last dimension, each value on 1 to 128 neighbouring positions
- gain: bfloat16 [16, 4096], P('blk', 'fsdp'), may hold values from 0.25 to 1.75
- qkv: bfloat16 [16, 4096, 768], P('blk', 'fsdp')
- proj: bfloat16 [16, 512, 4096], P('blk', None, 'fsdp'), may hold values from -0.25 to 0.25
- sum_gain: float32 [16, 4096], P('blk', 'fsdp'), may hold values from -6 to 6
- sum_qkv: float32 [16, 4096, 768], P('blk', 'fsdp'), may hold values from -6 to 6
- sum_proj: float32 [16, 512, 4096], P('blk', None, 'fsdp'), may hold values from -6 to 6
Outputs:
- hidden_out: bfloat16 [32768, 4096], P(('blk', 'fsdp'))
- new_sum_gain: float32 [16, 4096], P('blk', 'fsdp')
- new_sum_qkv: float32 [16, 4096, 768], P('blk', 'fsdp')
- new_sum_proj: float32 [16, 512, 4096], P('blk', None, 'fsdp')
The draws below stay inside these ranges and needn't reach their ends.
Inputs may be any that keep to these rules, and one draw needn't show every extreme that they name: `seg_forward`: each row of ids never falls along the micro-batch. `seg_backward`: each row of ids never falls along the micro-batch.
All inputs are finite; a program needn't handle non-finite values.
Results may differ from the reference program's by a relative error of at most 0.018.
The reference program's roundings to bfloat16 on the way count: a program that leaves them out, or rounds other values in their place, can miss the bound.
Values may be sent and summed in bfloat16 or wider, within the bound.
A program may use at most 192 MiB of HBM per device.

```python
import math
import jax
import jax.numpy as jnp
import numpy as np
from jax import lax

D = 4096
HEADS = 4
HEAD_DIM = 128
TOK_DEV = 256
SEGS = 4
QKV = 768
ATT = 512
MICRO = 128
TOKENS = 32768
N_BLK = 16
N_FSDP = 8


def scaled_rows(key, row_count, col_count):
    base_key, row_key, col_key = jax.random.split(key, 3)
    base_draw = jax.random.normal(base_key, (row_count, col_count), jnp.float32)
    row_scale = jnp.exp(jax.random.uniform(row_key, (row_count, 1), jnp.float32, math.log(0.3), math.log(3.0)))
    col_scale = jnp.exp(jax.random.uniform(col_key, (1, col_count), jnp.float32, math.log(0.3), math.log(3.0)))
    return (base_draw * row_scale * col_scale).astype(jnp.bfloat16)


def projection_draw(key):
    weight_key = jax.random.fold_in(key, 0)
    weights = jax.random.normal(weight_key, (N_BLK, D, QKV), jnp.float32) * D ** (-0.5)
    return weights.astype(jnp.bfloat16)


def draw_x_forward(key, part):
    return scaled_rows(jax.random.fold_in(key, 11), TOKENS, D)


def draw_x_saved(key, part):
    return scaled_rows(jax.random.fold_in(key, 13), TOKENS, D)


def draw_x_earlier(key, part):
    return scaled_rows(jax.random.fold_in(key, 17), TOKENS, D)


def draw_qkv(key, part):
    return projection_draw(jax.random.fold_in(key, 31))


def steps_of(rng, dims, cuts, low, top_value):
    def one(dim, parts):
        heights = jax.random.uniform(jax.random.fold_in(jax.random.fold_in(rng, 6), dim), (parts,), jnp.float32, low / len(cuts), top_value / len(cuts))
        return jnp.repeat(jnp.exp(heights), dims[dim] // parts).reshape((-1,) + (1,) * (len(dims) - dim - 1))

    level = one(*cuts[0])
    for cut in cuts[1:]:
        level = level * one(*cut)
    return level


def profile(number_of, total, limit, lean):
    weights = [(1 << 20) // math.isqrt(standing ** lean) + 1 for standing in range(2, number_of + 1)]
    surplus, given = total - limit - (number_of - 1), [1] * (number_of - 1)
    while surplus > 0:
        movable = [i for i in range(number_of - 1) if given[i] < limit]
        whole, remaining = sum([weights[i] for i in movable]), surplus
        for i in movable:
            extra = min(limit - given[i], max(1, remaining * weights[i] // whole), surplus)
            given[i] = given[i] + extra
            surplus = surplus - extra
    return np.array([limit] + given)


def ragged(stream_key, count, total, limit, skew):
    if count == 2:
        one = jax.random.randint(stream_key, (), max(1, total - limit), min(limit, total - 1) + 1)
        return jnp.stack([one, total - one])
    lengths = jnp.asarray(profile(count, total, limit, skew), jnp.int32)
    couples = (count - 1) // 2
    source_of, sink = lengths[1:1 + 2 * couples:2], lengths[2:2 + 2 * couples:2]
    room = jnp.minimum(source_of - 1, limit - sink)
    shifted = jax.random.randint(jax.random.fold_in(stream_key, 1), (couples,), 0, 1 << 20) % (room + 1)
    lengths = lengths.at[1:1 + 2 * couples:2].set(source_of - shifted).at[2:2 + 2 * couples:2].set(sink + shifted)
    return lengths[jax.random.permutation(jax.random.fold_in(stream_key, 2), count)]


def bell_draw(key, dims, deviation, bound, cuts=(), held_as=jnp.bfloat16):
    loudness = steps_of(key, dims, cuts, -0.22, 0.18) if cuts else 1.0
    entries = jax.random.normal(key, dims, jnp.float32) * deviation * loudness
    return jnp.minimum(jnp.maximum(entries, -bound), bound).astype(held_as)


def setup_inputs(seed: int = 0) -> dict:
    seeds = jax.random.split(jax.random.key(seed), 13)
    return {
        "x_forward": draw_x_forward(jax.random.fold_in(seeds[12], 71), 0),
        "seg_forward": jax.vmap(lambda own: jnp.searchsorted(jnp.cumsum(ragged(own, SEGS, TOK_DEV, TOK_DEV // 2, 0)), jnp.arange(TOK_DEV), side="right"))(jax.random.split(seeds[1], MICRO)).reshape((MICRO, TOK_DEV)).astype(jnp.int32),
        "x_saved": draw_x_saved(jax.random.fold_in(seeds[12], 71), 0),
        "x_earlier": draw_x_earlier(jax.random.fold_in(seeds[12], 71), 0),
        "cotangent": bell_draw(seeds[4], (TOKENS, D), 0.02, 0.119628906, ((0, 128),)),
        "seg_backward": jax.vmap(lambda own: jnp.searchsorted(jnp.cumsum(ragged(own, SEGS, TOK_DEV, TOK_DEV // 2, 0)), jnp.arange(TOK_DEV), side="right"))(jax.random.split(seeds[5], MICRO)).reshape((MICRO, TOK_DEV)).astype(jnp.int32),
        "gain": jnp.clip(1.0 + 0.15 * jax.random.normal(seeds[6], (N_BLK, D), jnp.float32), 0.25, 1.75).astype(jnp.bfloat16),
        "qkv": draw_qkv(jax.random.fold_in(seeds[12], 71), 0),
        "proj": bell_draw(seeds[8], (N_BLK, ATT, D), ATT ** -0.5, 0.25, ((0, 16), (2, 8))),
        "sum_gain": bell_draw(seeds[9], (N_BLK, D), 1.0, 6.0, ((0, 16), (1, 8)), jnp.float32),
        "sum_qkv": bell_draw(seeds[10], (N_BLK, D, QKV), 1.0, 6.0, ((0, 16), (1, 8)), jnp.float32),
        "sum_proj": bell_draw(seeds[11], (N_BLK, ATT, D), 1.0, 6.0, ((0, 16), (2, 8)), jnp.float32),
    }


def attention_mask(segments):
    count = segments.shape[0]
    row_ids = lax.broadcasted_iota(jnp.int32, (count, count), 0)
    col_ids = lax.broadcasted_iota(jnp.int32, (count, count), 1)
    return (col_ids <= row_ids) & (segments[:, None] == segments[None, :])

def layer_parts(tokens, segments, norm_gain, qkv_weight):
    count = tokens.shape[0]
    att_width = HEADS * HEAD_DIM
    wide_rows = tokens.astype(jnp.float32)
    inv_rms = lax.rsqrt(lax.optimization_barrier(jnp.mean(wide_rows * wide_rows, axis=1, keepdims=True)) + 1e-05)
    normed = (wide_rows * inv_rms * norm_gain.astype(jnp.float32)[None, :]).astype(jnp.bfloat16)
    projected = jnp.dot(normed, qkv_weight, preferred_element_type=jnp.float32).astype(jnp.bfloat16)
    queries = projected[:, :att_width].reshape(count, HEADS, HEAD_DIM)
    key_rows = projected[:, att_width:att_width + HEAD_DIM]
    values = projected[:, att_width + HEAD_DIM:]
    score_scale = HEAD_DIM ** (-0.5)
    scores = jnp.einsum('thd,sd->hts', queries.astype(jnp.float32), key_rows.astype(jnp.float32)) * score_scale
    allowed = attention_mask(segments)[None]
    scores = jnp.where(allowed, scores, -1e+30)
    row_max = lax.optimization_barrier(jnp.max(scores, axis=2, keepdims=True))
    expo = jnp.where(allowed, jnp.exp(scores - row_max), 0.0)
    attn_probs = expo / lax.optimization_barrier(jnp.sum(expo, axis=2, keepdims=True))
    attn_low = attn_probs.astype(jnp.bfloat16)
    attended = jnp.einsum('hts,sd->thd', attn_low.astype(jnp.float32), values.astype(jnp.float32))
    attended = attended.reshape(count, att_width).astype(jnp.bfloat16)
    return (wide_rows, inv_rms, normed, queries, key_rows, values, attn_probs, attn_low, attended)

def layer_forward(tokens, segments, layer_weights):
    norm_gain, qkv_weight, proj_weight = layer_weights
    pieces_all = layer_parts(tokens, segments, norm_gain, qkv_weight)
    branch_out = jnp.dot(pieces_all[8], proj_weight, preferred_element_type=jnp.float32)
    return (pieces_all[0] + branch_out).astype(jnp.bfloat16)

def layer_backward(tokens, segments, layer_weights, upstream, with_input):
    norm_gain, qkv_weight, proj_weight = layer_weights
    wide_rows, inv_rms, normed, queries, key_rows, values, attn_probs, attn_low, attended = layer_parts(tokens, segments, norm_gain, qkv_weight)
    count = tokens.shape[0]
    d_att = lax.dot_general(upstream, proj_weight, (((1,), (1,)), ((), ())), preferred_element_type=jnp.float32).astype(jnp.bfloat16)
    grad_proj = lax.dot_general(attended, upstream, (((0,), (0,)), ((), ())), preferred_element_type=jnp.float32)
    d_heads = d_att.reshape(count, HEADS, HEAD_DIM).astype(jnp.float32)
    d_probs = jnp.einsum('thd,sd->hts', d_heads, values.astype(jnp.float32))
    grad_values = jnp.einsum('hts,thd->sd', attn_low.astype(jnp.float32), d_heads)
    row_inner = lax.optimization_barrier(jnp.sum(d_probs * attn_probs, axis=2, keepdims=True))
    d_scores = (attn_probs * (d_probs - row_inner) * HEAD_DIM ** (-0.5)).astype(jnp.bfloat16)
    grad_queries = jnp.einsum('hts,sd->thd', d_scores.astype(jnp.float32), key_rows.astype(jnp.float32)).reshape(count, HEADS * HEAD_DIM)
    grad_keys = jnp.einsum('hts,thd->sd', d_scores.astype(jnp.float32), queries.astype(jnp.float32))
    d_projected = jnp.concatenate([grad_queries, grad_keys, grad_values], axis=1).astype(jnp.bfloat16)
    grad_qkv = lax.dot_general(normed, d_projected, (((0,), (0,)), ((), ())), preferred_element_type=jnp.float32)
    d_normed = lax.dot_general(d_projected, qkv_weight, (((1,), (1,)), ((), ())), preferred_element_type=jnp.float32)
    grad_gain = lax.optimization_barrier(jnp.sum(d_normed * wide_rows * inv_rms, axis=0))
    grad_terms = (grad_gain, grad_qkv, grad_proj)
    if not with_input:
        return (grad_terms, upstream)
    scaled = d_normed * norm_gain.astype(jnp.float32)[None, :]
    d_wide = inv_rms * scaled - wide_rows * inv_rms ** 3 * lax.optimization_barrier(jnp.mean(scaled * wide_rows, axis=1, keepdims=True))
    d_tokens = (upstream.astype(jnp.float32) + d_wide).astype(jnp.bfloat16)
    return (grad_terms, d_tokens)

def pick_layer(stack, cycle_pos):
    return lax.dynamic_index_in_dim(stack, cycle_pos, 0, keepdims=False)

def reference(x_forward, seg_forward, x_saved, x_earlier, cotangent, seg_backward, gain, qkv, proj, sum_gain, sum_qkv, sum_proj):

    def per_shard(cycle_pos, shard_pos):
        dev_index = cycle_pos * N_FSDP + shard_pos
        start_row = dev_index * TOK_DEV
        rows_fwd = lax.dynamic_slice_in_dim(x_forward, start_row, TOK_DEV, 0)
        rows_saved = lax.dynamic_slice_in_dim(x_saved, start_row, TOK_DEV, 0)
        rows_early = lax.dynamic_slice_in_dim(x_earlier, start_row, TOK_DEV, 0)
        rows_cot = lax.dynamic_slice_in_dim(cotangent, start_row, TOK_DEV, 0)
        ids_fwd = pick_layer(seg_forward, dev_index)
        ids_bwd = pick_layer(seg_backward, dev_index)
        before_pos = (cycle_pos + N_BLK - 1) % N_BLK
        layer_now = (pick_layer(gain, cycle_pos), pick_layer(qkv, cycle_pos), pick_layer(proj, cycle_pos))
        layer_next = (pick_layer(gain, before_pos), pick_layer(qkv, before_pos), pick_layer(proj, before_pos))
        hidden = layer_forward(rows_fwd, ids_fwd, layer_now)
        result = layer_forward(hidden, ids_fwd, layer_next)
        terms_one, d_hidden = layer_backward(rows_saved, ids_bwd, layer_now, rows_cot, True)
        terms_two, unused = layer_backward(rows_early, ids_bwd, layer_next, d_hidden, False)
        return (result, tuple((term.astype(jnp.bfloat16) for term in terms_one)), tuple((term.astype(jnp.bfloat16) for term in terms_two)))

    def per_cycle(cycle_pos):
        results, terms_one, terms_two = lax.map(lambda shard_pos: per_shard(cycle_pos, shard_pos), jnp.arange(N_FSDP, dtype=jnp.int32))
        sums_one = tuple((lax.optimization_barrier(jnp.sum(term.astype(jnp.float32), axis=0)) for term in terms_one))
        sums_two = tuple((lax.optimization_barrier(jnp.sum(term.astype(jnp.float32), axis=0)) for term in terms_two))
        return (results, sums_one, sums_two)
    results, sums_one, sums_two = lax.map(per_cycle, jnp.arange(N_BLK, dtype=jnp.int32))
    hidden_out = results.reshape(N_BLK * N_FSDP * TOK_DEV, D)
    new_sum_gain = jnp.roll(sum_gain + sums_one[0], 1, axis=0) + sums_two[0]
    new_sum_qkv = jnp.roll(sum_qkv + sums_one[1], 1, axis=0) + sums_two[1]
    new_sum_proj = jnp.roll(sum_proj + sums_one[2], 1, axis=0) + sums_two[2]
    return (hidden_out, new_sum_gain, new_sum_qkv, new_sum_proj)
```

```python
import functools

import jax
import jax.numpy as jnp
from jax import lax
from jax.experimental import pallas as pl
from jax.experimental.pallas import tpu as pltpu
from jax.sharding import PartitionSpec as P

HEADS = 4
PAD = 16
VMEM_LIMIT = 64 * 1024 * 1024 - 256 * 1024
MESH = pl.DeviceIdType.MESH
F32, BF16 = jnp.float32, jnp.bfloat16

MESSAGES = (
    "xe", "seg", "pR", "pL", "qZ", "qR", "qL", "pZ0", "pZ1", "pZ2", "pZ3", "pRf", "pLf", "cR", "cL",
    "eR", "eL", "dh0", "dh1", "dh2", "dh3", "hid", "res", "m1R", "m1L", "m2R", "m2L", "m3R", "m3L",
    "mZ0", "mZ1", "z0", "z1", "z2", "z3", "p1R", "p1L", "p2R", "p2L", "p3R", "p3L", "fq0", "fq1", "fp",
)
LOADS = (
    "wq", "wg", "wp", "xs", "xf", "cot", "sf", "sb", "sg", "sq", "sp", "oq0", "oq1", "op", "og",
)


def dot(a, b):
    return lax.dot_general(a, b, (((1,), (0,)), ((), ())), preferred_element_type=F32)


def dot_nt(a, b):
    return lax.dot_general(a, b, (((1,), (1,)), ((), ())), preferred_element_type=F32)


def dot_tn(a, b):
    return lax.dot_general(a, b, (((0,), (0,)), ((), ())), preferred_element_type=F32)


def kernel(
    n_blk, xf_in, xs_in, xe_in, cot_in, sf_in, sb_in, qkv_in, gain_in, proj_in, sg_in, sq_in, sp_in,
    out_h, out_g, out_q, out_p,
    Wq, Wp, Gq, Gp, RQ, RPZ, RPX, X, XE, COT, HID, DH, DN, NS, ACC, PR, ATTN, ATT_T, PROBS, DP, DATT, DACC,
    MASK, GK, GV, INV, CO, GG, SEGI, SEG, GN, SG, SQ, SP, FQ, FP, go, send_sem, recv_sem, load_sem,
):
    T, D = COT.shape
    C = Wq.shape[1] - PAD
    Q = Wq.shape[2]
    A = Wp.shape[1]
    HD = A // HEADS
    H2 = A // 2
    scale = HD ** (-0.5)

    b, f = lax.axis_index("blk"), lax.axis_index("fsdp")
    z, x = lax.div(f, 4), lax.rem(f, 4)
    odd = lax.rem(b, 2)

    def at(zz, xx):
        return lax.rem(zz, 2) * 4 + lax.rem(xx, 4)

    own, jL, jR, jF = f, at(z, x + 3), at(z, x + 1), at(z, x + 2)
    oz, ozL, ozR, ozF = at(z + 1, x), at(z + 1, x + 3), at(z + 1, x + 1), at(z + 1, x + 2)
    right, left, across = (b, jR), (b, jL), (b, oz)
    prev = (lax.rem(b + n_blk - 1, n_blk), lax.rem(f + 4 * (1 - odd), 8))
    following = (lax.rem(b + 1, n_blk), lax.rem(f + 4 * odd, 8))
    z_keep, z_send = z + odd, z + 1 + odd

    started = []

    def remote(name, src, dst, device):
        k = MESSAGES.index(name)
        return pltpu.make_async_remote_copy(
            src_ref=src, dst_ref=dst, send_sem=send_sem.at[k], recv_sem=recv_sem.at[k],
            device_id=device, device_id_type=MESH,
        )

    def send(name, src, dst, device):
        copy = remote(name, src, dst, device)
        copy.start()
        started.append(copy)

    def arrived(name, dst):
        remote(name, dst, dst, right).wait_recv()

    loads = {}

    def load(name, src, dst):
        loads[name] = pltpu.make_async_copy(src, dst, load_sem.at[LOADS.index(name)])
        loads[name].start()

    def cols(j):
        return pl.ds(pl.multiple_of(j * C, C), C)

    def wide(v):
        return jnp.concatenate([v] * (C // v.shape[1]), axis=1) if C > v.shape[1] else v

    def folded(v):
        total = v[:, 0:128]
        for k in range(1, v.shape[1] // 128):
            total = total + v[:, k * 128 : (k + 1) * 128]
        return total

    load("wp", proj_in, Wp.at[own])
    load("wq", qkv_in, Wq.at[own, pl.ds(0, C)])
    load("wg", gain_in, GN)
    load("sf", sf_in, SEGI.at[0])
    load("sb", sb_in, SEGI.at[1])
    load("xs", xs_in, X.at[0])
    load("xf", xf_in, X.at[1])
    load("cot", cot_in, COT)
    load("sg", sg_in, SG)
    load("sq", sq_in, SQ)
    load("sp", sp_in, SP)
    barrier = pltpu.get_barrier_semaphore()
    for device in (right, left, across, prev, following):
        pl.semaphore_signal(barrier, inc=1, device_id=device, device_id_type=MESH)
    loads["wg"].wait()
    loads["sf"].wait()
    loads["sb"].wait()
    loads["wp"].wait()
    loads["wq"].wait()
    Wq[own, C : C + PAD, 0:C] = jnp.broadcast_to(GN[...].astype(F32), (PAD, C)).astype(BF16)
    Wq[own, C : C + PAD, C:Q] = jnp.zeros((PAD, Q - C), BF16)
    SEG[0, 0] = jnp.broadcast_to(SEGI[0].astype(F32), (8, T))
    SEG[0, 1] = jnp.broadcast_to(SEGI[1].astype(F32), (8, T))
    pl.semaphore_wait(barrier, 5)

    send("xe", xe_in, XE, prev)
    send("seg", SEG.at[0], SEG.at[1], prev)

    @pl.when(odd == 1)
    def _():
        pl.semaphore_wait(go, 1)

    send("pR", Wp.at[own], Wp.at[own], right)
    send("pL", Wp.at[own], Wp.at[own], left)
    send("qZ", Wq.at[own], Wq.at[own], across)
    send("qR", Wq.at[own], Wq.at[own], right)
    send("qL", Wq.at[own], Wq.at[own], left)
    send("pZ0", Wp.at[own], Wp.at[own], across)

    def make_mask(place, kind, slot):
        row = jnp.broadcast_to(SEG[place, kind, 0:1, :], (T, T))
        col = row.T
        i = lax.broadcasted_iota(jnp.int32, (T, T), 0)
        j = lax.broadcasted_iota(jnp.int32, (T, T), 1)
        MASK[slot] = jnp.where((j <= i) & (row == col), 1.0, 0.0)

    def rms(read, slot):
        def step(j, total):
            v = read(cols(j)).astype(F32)
            return total + folded(v * v)

        total = lax.fori_loop(0, 8, step, jnp.zeros((T, 128), F32))
        inv = lax.rsqrt(jnp.sum(total, axis=1, keepdims=True) * (1.0 / D) + 1e-05)
        INV[slot] = jnp.broadcast_to(inv, (T, 128))

    def gain_row(j):
        return Wq[j, C : C + PAD, 0:C][0:1, :].astype(F32)

    def normed(read, slot, j):
        v = read(cols(j)).astype(F32)
        return (v * wide(INV[slot]) * gain_row(j)).astype(BF16)

    def read_s(c):
        return X[0, :, c]

    def read_f(c):
        return X[1, :, c]

    def read_e(c):
        return XE[:, c]

    def read_h(c):
        return HID[:, c]

    def project_piece(j):
        for i, read in ((0, read_s), (1, read_f), (2, read_e)):
            block = normed(read, i, j)
            if i == 0:
                NS[j] = block
            ACC[i] += dot(block, Wq[j, 0:C, :])

    def project_all(read, slot, dst):
        rms(read, slot)
        ACC[0] = jnp.zeros((T, Q), F32)

        def step(j, carry):
            ACC[0] += dot(normed(read, slot, j), Wq[j, 0:C, :])
            return carry

        lax.fori_loop(0, 8, step, 0)
        PR[dst] = ACC[0].astype(BF16)

    def head(h):
        return slice(h * HD, (h + 1) * HD)

    def attention(src, mask_slot, probs, t_off):
        def step(h, carry):
            allowed = MASK[mask_slot] > 0.5
            s = dot_nt(PR[src, :, head(h)], PR[src, :, A : A + HD]) * scale
            s = jnp.where(allowed, s, -1e30)
            e = jnp.where(allowed, jnp.exp(s - jnp.max(s, axis=1, keepdims=True)), 0.0)
            p = e / jnp.sum(e, axis=1, keepdims=True)
            if probs:
                PROBS[h] = p
            out = dot(p.astype(BF16), PR[src, :, A + HD : A + 2 * HD])
            if probs:
                ATT_T[head(h), t_off : t_off + T] = out.T.astype(BF16)
            else:
                ATTN[:, head(h)] = out.astype(BF16)
            return carry

        for h in range(HEADS):
            step(h, 0)

    def attention_back(src, dst):
        GK[...] = jnp.zeros_like(GK)
        GV[...] = jnp.zeros_like(GV)

        def step(h, carry):
            d_head = DATT[:, head(h)]
            p = PROBS[h]
            dp = dot_nt(d_head, PR[src, :, A + HD : A + 2 * HD])
            inner = jnp.sum(dp * p, axis=1, keepdims=True)
            ds = (p * (dp - inner) * scale).astype(BF16)
            DP[dst, :, head(h)] = dot(ds, PR[src, :, A : A + HD]).astype(BF16)
            GK[...] += dot_tn(ds, PR[src, :, head(h)])
            GV[...] += dot_tn(p.astype(BF16), d_head)
            return carry

        for h in range(HEADS):
            step(h, 0)
        DP[dst, :, A : A + HD] = GK[...].astype(BF16)
        DP[dst, :, A + HD : A + 2 * HD] = GV[...].astype(BF16)

    def d_att_piece(j):
        DACC[...] += dot_nt(COT[:, cols(j)], Wp[j])

    make_mask(0, 1, 0)
    make_mask(0, 0, 1)
    for j in range(8):
        Gq[j, C : C + PAD, :] = jnp.zeros((PAD, Q), BF16)
    ACC[...] = jnp.zeros_like(ACC)
    DACC[...] = jnp.zeros_like(DACC)
    loads["xs"].wait()
    rms(read_s, 0)
    loads["xf"].wait()
    rms(read_f, 1)
    loads["cot"].wait()
    arrived("seg", SEG.at[1])
    make_mask(1, 1, 2)
    make_mask(1, 0, 3)

    arrived("pR", Wp.at[jL])
    send("pRf", Wp.at[jL, pl.ds(0, H2)], Wp.at[jL, pl.ds(0, H2)], right)
    send("pZ1", Wp.at[jL], Wp.at[jL], across)
    arrived("pL", Wp.at[jR])
    send("pLf", Wp.at[jR, pl.ds(H2, H2)], Wp.at[jR, pl.ds(H2, H2)], left)
    send("pZ2", Wp.at[jR], Wp.at[jR], across)
    arrived("qZ", Wq.at[oz])
    send("cR", Wq.at[oz], Wq.at[oz], right)
    send("cL", Wq.at[oz], Wq.at[oz], left)
    arrived("xe", XE)
    rms(read_e, 2)
    project_piece(own)
    arrived("pRf", Wp.at[jF, pl.ds(0, H2)])
    arrived("pLf", Wp.at[jF, pl.ds(H2, H2)])
    send("pZ3", Wp.at[jF], Wp.at[jF], across)
    arrived("qR", Wq.at[jL])
    send("eR", Wq.at[jL], Wq.at[jL], right)
    project_piece(oz)
    project_piece(jL)
    arrived("qL", Wq.at[jR])
    project_piece(jR)
    d_att_piece(own)
    d_att_piece(jL)
    d_att_piece(jR)
    d_att_piece(jF)
    arrived("cL", Wq.at[ozR])
    send("eL", Wq.at[ozR], Wq.at[ozR], left)

    @pl.when(odd == 0)
    def _():
        pl.semaphore_signal(go, inc=1, device_id=following, device_id_type=MESH)

    project_piece(ozR)
    arrived("cR", Wq.at[ozL])
    project_piece(ozL)
    arrived("pZ0", Wp.at[oz])
    d_att_piece(oz)
    arrived("pZ1", Wp.at[ozL])
    d_att_piece(ozL)
    arrived("pZ2", Wp.at[ozR])
    d_att_piece(ozR)
    arrived("eR", Wq.at[jF])
    project_piece(jF)
    arrived("eL", Wq.at[ozF])
    project_piece(ozF)
    PR[0] = ACC[0].astype(BF16)
    PR[1] = ACC[1].astype(BF16)
    PR[2] = ACC[2].astype(BF16)
    attention(0, 0, True, 0)
    arrived("pZ3", Wp.at[ozF])
    d_att_piece(ozF)
    DATT[...] = DACC[...].astype(BF16)

    attention_back(0, 0)

    def scaled_piece(j, total):
        d_normed = dot_nt(DP[0], Wq[j, 0:C, :])
        v = X[0, :, cols(j)].astype(F32)
        GG[j] = jnp.broadcast_to(jnp.sum(d_normed * (v * wide(INV[0])), axis=0, keepdims=True), (8, C))
        scaled = d_normed * gain_row(j)
        DN[j] = scaled
        return total + folded(scaled * v)

    total = lax.fori_loop(0, 8, scaled_piece, jnp.zeros((T, 128), F32))
    inv = INV[0]
    CO[...] = inv * inv * inv * (jnp.sum(total, axis=1, keepdims=True) * (1.0 / D))
    for k in range(4):
        rows = slice(k * (T // 4), (k + 1) * (T // 4))

        def dx_piece(j, carry):
            v = X[0, rows, cols(j)].astype(F32)
            d_wide = wide(INV[0, rows, :]) * DN[j, rows, :] - v * wide(CO[rows, :])
            X[0, rows, cols(j)] = (COT[rows, cols(j)].astype(F32) + d_wide).astype(BF16)
            return carry

        lax.fori_loop(0, 8, dx_piece, 0)
        send(f"dh{k}", X.at[0, pl.ds(k * (T // 4), T // 4)], DH.at[pl.ds(k * (T // 4), T // 4)], prev)

    hidden_copy = remote("hid", X.at[1], HID, prev)
    started.append(hidden_copy)

    def forward_one():
        attention(1, 1, False, 0)

        def out_piece(j, carry):
            X[1, :, cols(j)] = (X[1, :, cols(j)].astype(F32) + dot(ATTN[...], Wp[j])).astype(BF16)
            return carry

        lax.fori_loop(0, 8, out_piece, 0)
        hidden_copy.start()

    attention(2, 2, True, T)
    pl.when(odd == 0)(forward_one)
    loads["sg"].wait()
    loads["sq"].wait()
    loads["sp"].wait()

    for k in range(4):
        arrived(f"dh{k}", DH.at[pl.ds(k * (T // 4), T // 4)])

    DACC[...] = jnp.zeros_like(DACC)

    def d_att_two(j, carry):
        DACC[...] += dot_nt(DH[:, cols(j)], Wp[j])
        return carry

    lax.fori_loop(0, 8, d_att_two, 0)
    DATT[...] = DACC[...].astype(BF16)
    attention_back(2, 1)

    def is_own(j):
        return jnp.where(j == own, 1.0, 0.0)

    def grad_qkv(j):
        d_normed = dot_nt(DP[1], Wq[j, 0:C, :])
        xi = XE[:, cols(j)].astype(F32) * wide(INV[2])
        gg = GG[j][0:1, :] + jnp.sum(d_normed * xi, axis=0, keepdims=True)
        Gq[j, C : C + PAD, 0:C] = (jnp.broadcast_to(gg, (PAD, C)) + is_own(j) * SG[...]).astype(BF16)
        block = (xi * gain_row(j)).astype(BF16)
        terms = dot_tn(NS[j], DP[0]) + dot_tn(block, DP[1])
        Gq[j, 0:C, :] = (terms + is_own(j) * SQ[...]).astype(BF16)

    def grad_proj(j):
        terms = dot(ATT_T[:, 0:T], COT[:, cols(j)]) + dot(ATT_T[:, T : 2 * T], DH[:, cols(j)])
        Gp[j] = (terms + is_own(j) * SP[...]).astype(BF16)

    def each(count, work):
        def step(k, carry):
            work(k)
            return carry

        lax.fori_loop(0, count, step, 0)

    QR = 48 if (C + PAD) % 48 == 0 else 16

    def add_q(j, slots, first=0, last=C + PAD):
        def work(k):
            rows = pl.ds(pl.multiple_of(first + k * QR, 16), QR)
            v = Gq[j, rows, :].astype(F32)
            for s in slots:
                v = v + RQ[s, rows, :].astype(F32)
            Gq[j, rows, :] = v.astype(BF16)

        each((last - first) // QR, work)

    def add_p(j, base, size, parts):
        def work(k):
            off = pl.multiple_of(k * 16, 16)
            v = Gp[j, pl.ds(base + off, 16), :].astype(F32)
            for ref in parts:
                v = v + ref[pl.ds(off, 16), :].astype(F32)
            Gp[j, pl.ds(base + off, 16), :] = v.astype(BF16)

        each(size // 16, work)

    each(2, lambda k: grad_qkv(at(z + k, x + 2)))
    send("m1R", Gq.at[jF], RQ.at[0], right)
    send("m1L", Gq.at[ozF], RQ.at[1], left)
    each(4, lambda k: grad_proj(at(z_send, k)))
    for q, off in enumerate((2, 1, 3, 0)):
        send(f"z{q}", Gp.at[at(z_send, x + off)], RPZ.at[q], across)
    each(2, lambda k: grad_qkv(at(z + 1 + k, x + 1 + 2 * k)))
    send("m2R", Gq.at[ozR], RQ.at[2], right)
    send("m2L", Gq.at[jL], RQ.at[3], left)
    pl.when(odd == 1)(forward_one)
    each(2, lambda k: grad_qkv(at(z + k, x + 1 + 2 * k)))
    each(2, lambda k: grad_qkv(at(z + k, x)))
    each(4, lambda k: grad_proj(at(z_keep, k)))
    arrived("m1R", RQ.at[0])
    add_q(jR, (0,))
    send("m3R", Gq.at[jR], RQ.at[4], right)
    arrived("m1L", RQ.at[1])
    add_q(ozL, (1,))
    send("m3L", Gq.at[ozL], RQ.at[5], left)

    arrived("hid", HID)
    project_all(read_h, 3, 1)
    attention(1, 3, False, 0)

    def result_piece(j, carry):
        HID[:, cols(j)] = (HID[:, cols(j)].astype(F32) + dot(ATTN[...], Wp[j])).astype(BF16)
        return carry

    lax.fori_loop(0, 8, result_piece, 0)
    send("res", HID, out_h, following)

    kF, kR, kL, kO = (at(z_keep, x + off) for off in (2, 1, 3, 0))
    top, low = pl.ds(0, H2), pl.ds(H2, H2)
    arrived("z0", RPZ.at[0])
    add_p(kF, 0, A, (RPZ.at[0],))
    send("p1R", Gp.at[kF, top], RPX.at[0], right)
    send("p1L", Gp.at[kF, low], RPX.at[1], left)
    arrived("z1", RPZ.at[1])
    add_p(kR, 0, A, (RPZ.at[1],))
    send("p2R", Gp.at[kR, low], RPX.at[2], right)
    arrived("z2", RPZ.at[2])
    add_p(kL, 0, A, (RPZ.at[2],))
    send("p2L", Gp.at[kL, top], RPX.at[3], left)
    arrived("m2R", RQ.at[2])
    arrived("m2L", RQ.at[3])
    arrived("m3R", RQ.at[4])
    arrived("m3L", RQ.at[5])
    j_send, j_keep = at(z_send, x), at(z_keep, x)
    cut = (C + PAD) // QR // 2 * QR
    part0, part1 = pl.ds(0, cut), pl.ds(cut, C + PAD - cut)
    add_q(j_send, (2 + odd, 5 - odd))
    send("mZ0", Gq.at[j_send, part0], RQ.at[6, part0], across)
    send("mZ1", Gq.at[j_send, part1], RQ.at[6, part1], across)
    arrived("p1R", RPX.at[0])
    add_p(kR, 0, H2, (RPX.at[0],))
    send("p3R", Gp.at[kR, top], RPX.at[4], right)
    arrived("p1L", RPX.at[1])
    add_p(kL, H2, H2, (RPX.at[1],))
    send("p3L", Gp.at[kL, low], RPX.at[5], left)
    add_q(j_keep, (3 - odd, 4 + odd))
    arrived("z3", RPZ.at[3])
    arrived("p2R", RPX.at[2])
    arrived("p2L", RPX.at[3])
    arrived("p3R", RPX.at[4])
    arrived("p3L", RPX.at[5])
    add_p(kO, 0, H2, (RPZ.at[3, top], RPX.at[4], RPX.at[3]))
    add_p(kO, H2, H2, (RPZ.at[3, low], RPX.at[2], RPX.at[5]))
    send("fp", Gp.at[kO], FP, following)
    arrived("mZ0", RQ.at[6, part0])
    add_q(j_keep, (6,), 0, cut)
    send("fq0", Gq.at[j_keep, part0], FQ.at[part0], following)
    arrived("mZ1", RQ.at[6, part1])
    add_q(j_keep, (6,), cut)
    send("fq1", Gq.at[j_keep, part1], FQ.at[part1], following)

    arrived("fp", FP)
    SP[...] = FP[...].astype(F32)
    load("op", SP, out_p)
    arrived("fq0", FQ.at[part0])
    SQ[0:cut, :] = FQ[0:cut, :].astype(F32)
    load("oq0", SQ.at[part0], out_q.at[part0])
    arrived("fq1", FQ.at[part1])
    SG[...] = FQ[C : C + PAD, 0:C].astype(F32)[0:1, :]
    load("og", SG, out_g)
    SQ[cut:C, :] = FQ[cut:C, :].astype(F32)
    load("oq1", SQ.at[pl.ds(cut, C - cut)], out_q.at[pl.ds(cut, C - cut)])
    arrived("res", out_h)
    for name in ("op", "oq0", "og", "oq1"):
        loads[name].wait()
    for copy in started:
        copy.wait_send()


def body(
    n_blk, x_forward, seg_forward, x_saved, x_earlier, cotangent, seg_backward,
    gain, qkv, proj, sum_gain, sum_qkv, sum_proj,
):
    T, D = x_forward.shape
    C, Q = qkv.shape[1:]
    A = proj.shape[1]
    HD = A // HEADS
    anywhere = pl.BlockSpec(memory_space=pl.ANY)
    V = pltpu.VMEM
    scratch = [
        V((8, C + PAD, Q), BF16), V((8, A, C), BF16), V((8, C + PAD, Q), BF16), V((8, A, C), BF16),
        V((7, C + PAD, Q), BF16), V((4, A, C), BF16), V((6, A // 2, C), BF16),
        V((2, T, D), BF16), V((T, D), BF16), V((T, D), BF16), V((T, D), BF16), V((T, D), BF16),
        V((8, T, C), F32), V((8, T, C), BF16), V((3, T, Q), F32), V((3, T, Q), BF16),
        V((T, A), BF16), V((A, 2 * T), BF16), V((HEADS, T, T), F32), V((2, T, Q), BF16),
        V((T, A), BF16), V((T, A), F32), V((4, T, T), F32), V((T, HD), F32), V((T, HD), F32),
        V((4, T, 128), F32), V((T, 128), F32), V((8, 8, C), F32), V((2, 1, T), jnp.int32),
        V((2, 2, 8, T), F32), V((1, C), BF16), V((1, C), F32), V((C, Q), F32), V((A, C), F32),
        V((C + PAD, Q), BF16), V((A, C), BF16), pltpu.SemaphoreType.REGULAR,
        pltpu.SemaphoreType.DMA((len(MESSAGES),)),
        pltpu.SemaphoreType.DMA((len(MESSAGES),)),
        pltpu.SemaphoreType.DMA((len(LOADS),)),
    ]
    hidden, new_g, new_q, new_p = pl.pallas_call(
        functools.partial(kernel, n_blk),
        out_shape=(
            jax.ShapeDtypeStruct((T, D), BF16),
            jax.ShapeDtypeStruct((1, C), F32),
            jax.ShapeDtypeStruct((C, Q), F32),
            jax.ShapeDtypeStruct((A, C), F32),
        ),
        in_specs=[anywhere] * 12,
        out_specs=(anywhere,) * 4,
        scratch_shapes=scratch,
        compiler_params=pltpu.CompilerParams(
            collective_id=0, has_side_effects=True, vmem_limit_bytes=VMEM_LIMIT
        ),
        name="two_steps",
    )(
        x_forward, x_saved, x_earlier, cotangent, seg_forward, seg_backward, qkv[0], gain, proj[0],
        sum_gain, sum_qkv[0], sum_proj[0],
    )
    return hidden, new_g, new_q[None], new_p[None]


def solution(mesh):
    rows, layer = P(("blk", "fsdp"), None), P("blk", "fsdp")
    q_spec, p_spec = P("blk", "fsdp", None), P("blk", None, "fsdp")
    return jax.shard_map(
        functools.partial(body, mesh.shape["blk"]),
        mesh=mesh,
        in_specs=(rows,) * 6 + (layer, q_spec, p_spec) * 2,
        out_specs=(rows, layer, q_spec, p_spec),
        check_vma=False,
    )
```

```python
import functools

import jax
import jax.numpy as jnp
from jax import lax
from jax.experimental import pallas as pl
from jax.experimental.pallas import tpu as pltpu
from jax.sharding import PartitionSpec as P

HEADS = 4
PAD = 16
VMEM_LIMIT = 64 * 1024 * 1024 - 256 * 1024
MESH = pl.DeviceIdType.MESH
F32, BF16 = jnp.float32, jnp.bfloat16

MESSAGES = (
    "xe", "seg", "pR", "pL", "pZ0", "pZ1", "pZ2", "pZ3", "pRf", "pLf", "dh0", "dh1", "dh2", "dh3",
    "hid", "res", "z0", "z1", "z2", "z3", "p1R", "p1L", "p2R", "p2L", "p3R", "p3L", "fp", "qZ_0",
    "qZ_1", "qR_0", "qR_1", "qL_0", "qL_1", "cR_0", "cR_1", "cL_0", "cL_1", "eR_0", "eR_1", "eL_0",
    "eL_1", "m1R_0", "m1R_1", "m1L_0", "m1L_1", "m2R_0", "m2R_1", "m2L_0", "m2L_1", "m3R_0",
    "m3R_1", "m3L_0", "m3L_1", "mZ_0", "mZ_1", "fq_0", "fq_1",
)
LOADS = (
    "wq", "wg", "wp", "xs", "xf", "cot", "sf", "sb", "sg", "sq", "sp",
)


def dot(a, b):
    return lax.dot_general(a, b, (((1,), (0,)), ((), ())), preferred_element_type=F32)


def dot_nt(a, b):
    return lax.dot_general(a, b, (((1,), (1,)), ((), ())), preferred_element_type=F32)


def dot_tn(a, b):
    return lax.dot_general(a, b, (((0,), (0,)), ((), ())), preferred_element_type=F32)


def kernel(
    n_blk, xf_in, xs_in, xe_in, cot_in, sf_in, sb_in, qkv_in, gain_in, proj_in, sg_in, sq_in, sp_in,
    out_h, out_q, out_p,
    Wq, Wp, Gq, Gp, RQ, RPZ, RPX, X, XE, COT, HID, DH, DN, NS, ACC, PR, ATTN, ATT_T, PROBS, DP, DATT, DACC,
    MASK, GK, GV, INV, CO, GG, SEGI, SEG, GN, SG, SQ, SP, go, turn, send_sem, recv_sem, load_sem,
):
    T, D = COT.shape
    C = Wq.shape[1] - PAD
    Q = Wq.shape[2]
    A = Wp.shape[1]
    HD = A // HEADS
    H2 = A // 2
    scale = HD ** (-0.5)
    QR = 48 if (C + PAD) % 48 == 0 else 16

    b, f = lax.axis_index("blk"), lax.axis_index("fsdp")
    z, x = lax.div(f, 4), lax.rem(f, 4)
    odd = lax.rem(b, 2)

    def at(zz, xx):
        return lax.rem(zz, 2) * 4 + lax.rem(xx, 4)

    own, jL, jR, jF = f, at(z, x + 3), at(z, x + 1), at(z, x + 2)
    oz, ozL, ozR, ozF = at(z + 1, x), at(z + 1, x + 3), at(z + 1, x + 1), at(z + 1, x + 2)
    right, left, across = (b, jR), (b, jL), (b, oz)
    prev = (lax.rem(b + n_blk - 1, n_blk), lax.rem(f + 4 * (1 - odd), 8))
    following = (lax.rem(b + 1, n_blk), lax.rem(f + 4 * odd, 8))
    z_keep, z_send = z + odd, z + 1 + odd

    started = []

    def remote(name, src, dst, device):
        k = MESSAGES.index(name)
        return pltpu.make_async_remote_copy(
            src_ref=src, dst_ref=dst, send_sem=send_sem.at[k], recv_sem=recv_sem.at[k],
            device_id=device, device_id_type=MESH,
        )

    def send(name, src, dst, device):
        copy = remote(name, src, dst, device)
        copy.start()
        started.append(copy)

    def arrived(name, dst):
        remote(name, dst, dst, right).wait_recv()

    cut = (C + PAD) // QR // 2 * QR
    spans = ((0, cut), (cut, C + PAD))
    parts = (pl.ds(0, cut), pl.ds(cut, C + PAD - cut))

    def send_part(name, k, src, dst, device):
        send(f"{name}_{k}", src.at[parts[k]], dst.at[parts[k]], device)

    def send_both(name, src, dst, device):
        for k in range(2):
            send_part(name, k, src, dst, device)

    def arrived_part(name, k, dst):
        arrived(f"{name}_{k}", dst.at[parts[k]])

    def arrived_both(name, dst):
        for k in range(2):
            arrived_part(name, k, dst)

    loads = {}

    def load(name, src, dst):
        loads[name] = pltpu.make_async_copy(src, dst, load_sem.at[LOADS.index(name)])
        loads[name].start()

    def cols(j):
        return pl.ds(pl.multiple_of(j * C, C), C)

    def wide(v):
        return jnp.concatenate([v] * (C // v.shape[1]), axis=1) if C > v.shape[1] else v

    def folded(v):
        total = v[:, 0:128]
        for k in range(1, v.shape[1] // 128):
            total = total + v[:, k * 128 : (k + 1) * 128]
        return total

    load("wp", proj_in, Wp.at[own])
    load("wq", qkv_in, Wq.at[own, pl.ds(0, C)])
    load("wg", gain_in, GN)
    load("sf", sf_in, SEGI.at[0])
    load("sb", sb_in, SEGI.at[1])
    load("xs", xs_in, X.at[0])
    load("xf", xf_in, X.at[1])
    load("cot", cot_in, COT)
    load("sg", sg_in, SG)
    load("sq", sq_in, SQ)
    load("sp", sp_in, SP)
    barrier = pltpu.get_barrier_semaphore()
    for device in (right, left, across, prev, following):
        pl.semaphore_signal(barrier, inc=1, device_id=device, device_id_type=MESH)
    loads["wg"].wait()
    loads["sf"].wait()
    loads["sb"].wait()
    SEG[0, 0] = jnp.broadcast_to(SEGI[0].astype(F32), (8, T))
    SEG[0, 1] = jnp.broadcast_to(SEGI[1].astype(F32), (8, T))
    loads["wq"].wait()
    Wq[own, C : C + PAD, 0:C] = jnp.broadcast_to(GN[...].astype(F32), (PAD, C)).astype(BF16)
    Wq[own, C : C + PAD, C:Q] = jnp.zeros((PAD, Q - C), BF16)
    loads["wp"].wait()
    pl.semaphore_wait(barrier, 5)

    send("xe", xe_in, XE, prev)
    send("seg", SEG.at[0], SEG.at[1], prev)

    def gather_starts():
        copies = [
            remote("pR", Wp.at[own], Wp.at[own], right),
            remote("pL", Wp.at[own], Wp.at[own], left),
        ]
        for name, device in (("qZ", across), ("qR", right)):
            for k in range(2):
                piece = Wq.at[own, parts[k]]
                copies.append(remote(f"{name}_{k}", piece, piece, device))
        return copies

    first_copies = gather_starts()
    started.extend(first_copies)

    @pl.when(odd == 0)
    def _():
        for copy in first_copies:
            copy.start()

    def make_mask(place, kind, slot):
        row = jnp.broadcast_to(SEG[place, kind, 0:1, :], (T, T))
        col = row.T
        i = lax.broadcasted_iota(jnp.int32, (T, T), 0)
        j = lax.broadcasted_iota(jnp.int32, (T, T), 1)
        MASK[slot] = jnp.where((j <= i) & (row == col), 1.0, 0.0)

    def rms(read, slot):
        def step(j, total):
            v = read(cols(j)).astype(F32)
            return total + folded(v * v)

        total = lax.fori_loop(0, 8, step, jnp.zeros((T, 128), F32))
        inv = lax.rsqrt(jnp.sum(total, axis=1, keepdims=True) * (1.0 / D) + 1e-05)
        INV[slot] = jnp.broadcast_to(inv, (T, 128))

    def gain_row(j):
        return Wq[j, C : C + PAD, 0:C][0:1, :].astype(F32)

    def normed(read, slot, j):
        v = read(cols(j)).astype(F32)
        return (v * wide(INV[slot]) * gain_row(j)).astype(BF16)

    def read_s(c):
        return X[0, :, c]

    def read_f(c):
        return X[1, :, c]

    def read_e(c):
        return XE[:, c]

    def read_h(c):
        return HID[:, c]

    def project_piece(j):
        for i, read in ((0, read_s), (1, read_f), (2, read_e)):
            block = normed(read, i, j)
            if i == 0:
                NS[j] = block
            ACC[i] += dot(block, Wq[j, 0:C, :])

    def project_all(read, slot, dst):
        rms(read, slot)
        ACC[0] = jnp.zeros((T, Q), F32)

        def step(j, carry):
            ACC[0] += dot(normed(read, slot, j), Wq[j, 0:C, :])
            return carry

        lax.fori_loop(0, 8, step, 0)
        PR[dst] = ACC[0].astype(BF16)

    def head(h):
        return slice(h * HD, (h + 1) * HD)

    def attention(src, mask_slot, probs, t_off):
        def step(h, carry):
            allowed = MASK[mask_slot] > 0.5
            s = dot_nt(PR[src, :, head(h)], PR[src, :, A : A + HD]) * scale
            s = jnp.where(allowed, s, -1e30)
            e = jnp.where(allowed, jnp.exp(s - jnp.max(s, axis=1, keepdims=True)), 0.0)
            p = e / jnp.sum(e, axis=1, keepdims=True)
            if probs:
                PROBS[h] = p
            out = dot(p.astype(BF16), PR[src, :, A + HD : A + 2 * HD])
            if probs:
                ATT_T[head(h), t_off : t_off + T] = out.T.astype(BF16)
            else:
                ATTN[:, head(h)] = out.astype(BF16)
            return carry

        for h in range(HEADS):
            step(h, 0)

    def attention_back(src, dst):
        GK[...] = jnp.zeros_like(GK)
        GV[...] = jnp.zeros_like(GV)

        def step(h, carry):
            d_head = DATT[:, head(h)]
            p = PROBS[h]
            dp = dot_nt(d_head, PR[src, :, A + HD : A + 2 * HD])
            inner = jnp.sum(dp * p, axis=1, keepdims=True)
            ds = (p * (dp - inner) * scale).astype(BF16)
            DP[dst, :, head(h)] = dot(ds, PR[src, :, A : A + HD]).astype(BF16)
            GK[...] += dot_tn(ds, PR[src, :, head(h)])
            GV[...] += dot_tn(p.astype(BF16), d_head)
            return carry

        for h in range(HEADS):
            step(h, 0)
        DP[dst, :, A : A + HD] = GK[...].astype(BF16)
        DP[dst, :, A + HD : A + 2 * HD] = GV[...].astype(BF16)

    def d_att_piece(j):
        DACC[...] += dot_nt(COT[:, cols(j)], Wp[j])

    make_mask(0, 1, 0)
    make_mask(0, 0, 1)
    for j in range(8):
        Gq[j, C : C + PAD, :] = jnp.zeros((PAD, Q), BF16)
    ACC[...] = jnp.zeros_like(ACC)
    DACC[...] = jnp.zeros_like(DACC)
    loads["xs"].wait()
    rms(read_s, 0)
    loads["xf"].wait()
    rms(read_f, 1)
    loads["cot"].wait()
    arrived("seg", SEG.at[1])
    make_mask(1, 1, 2)
    make_mask(1, 0, 3)

    @pl.when(odd == 1)
    def _():
        pl.semaphore_wait(go, 1)
        for copy in first_copies:
            copy.start()

    arrived_part("qZ", 0, Wq.at[oz])
    send_part("cL", 0, Wq.at[oz], Wq.at[oz], left)
    send_part("cR", 0, Wq.at[oz], Wq.at[oz], right)
    send("pZ0", Wp.at[own], Wp.at[own], across)
    arrived("pR", Wp.at[jL])
    send("pRf", Wp.at[jL, pl.ds(0, H2)], Wp.at[jL, pl.ds(0, H2)], right)
    send("pZ1", Wp.at[jL], Wp.at[jL], across)
    arrived("pL", Wp.at[jR])
    send("pLf", Wp.at[jR, pl.ds(H2, H2)], Wp.at[jR, pl.ds(H2, H2)], left)
    send("pZ2", Wp.at[jR], Wp.at[jR], across)
    arrived_part("qZ", 1, Wq.at[oz])
    send_part("cL", 1, Wq.at[oz], Wq.at[oz], left)
    send_part("cR", 1, Wq.at[oz], Wq.at[oz], right)
    send_both("qL", Wq.at[own], Wq.at[own], left)
    arrived_part("qR", 0, Wq.at[jL])
    send_part("eR", 0, Wq.at[jL], Wq.at[jL], right)
    arrived("xe", XE)
    rms(read_e, 2)
    project_piece(own)
    arrived_part("qR", 1, Wq.at[jL])
    send_part("eR", 1, Wq.at[jL], Wq.at[jL], right)
    arrived("pRf", Wp.at[jF, pl.ds(0, H2)])
    arrived("pLf", Wp.at[jF, pl.ds(H2, H2)])
    send("pZ3", Wp.at[jF], Wp.at[jF], across)
    project_piece(oz)
    project_piece(jL)
    arrived_part("cL", 0, Wq.at[ozR])
    send_part("eL", 0, Wq.at[ozR], Wq.at[ozR], left)
    arrived_both("qL", Wq.at[jR])
    project_piece(jR)
    arrived_part("cL", 1, Wq.at[ozR])
    send_part("eL", 1, Wq.at[ozR], Wq.at[ozR], left)

    @pl.when(odd == 0)
    def _():
        pl.semaphore_signal(go, inc=1, device_id=following, device_id_type=MESH)

    d_att_piece(own)
    d_att_piece(jL)
    d_att_piece(jR)
    d_att_piece(jF)
    project_piece(ozR)
    arrived_both("cR", Wq.at[ozL])
    project_piece(ozL)
    arrived("pZ0", Wp.at[oz])
    d_att_piece(oz)
    arrived("pZ1", Wp.at[ozL])
    d_att_piece(ozL)
    arrived("pZ2", Wp.at[ozR])
    d_att_piece(ozR)
    arrived_both("eR", Wq.at[jF])
    project_piece(jF)
    arrived_both("eL", Wq.at[ozF])
    project_piece(ozF)
    PR[0] = ACC[0].astype(BF16)
    PR[1] = ACC[1].astype(BF16)
    PR[2] = ACC[2].astype(BF16)
    attention(0, 0, True, 0)
    arrived("pZ3", Wp.at[ozF])
    d_att_piece(ozF)
    DATT[...] = DACC[...].astype(BF16)

    attention_back(0, 0)

    def scaled_piece(j, total):
        d_normed = dot_nt(DP[0], Wq[j, 0:C, :])
        v = X[0, :, cols(j)].astype(F32)
        GG[j] = jnp.broadcast_to(jnp.sum(d_normed * (v * wide(INV[0])), axis=0, keepdims=True), (8, C))
        scaled = d_normed * gain_row(j)
        DN[j] = scaled
        return total + folded(scaled * v)

    total = lax.fori_loop(0, 8, scaled_piece, jnp.zeros((T, 128), F32))
    inv = INV[0]
    CO[...] = inv * inv * inv * (jnp.sum(total, axis=1, keepdims=True) * (1.0 / D))
    for k in range(4):
        rows = slice(k * (T // 4), (k + 1) * (T // 4))

        def dx_piece(j, carry):
            v = X[0, rows, cols(j)].astype(F32)
            d_wide = wide(INV[0, rows, :]) * DN[j, rows, :] - v * wide(CO[rows, :])
            X[0, rows, cols(j)] = (COT[rows, cols(j)].astype(F32) + d_wide).astype(BF16)
            return carry

        lax.fori_loop(0, 8, dx_piece, 0)
        send(f"dh{k}", X.at[0, pl.ds(k * (T // 4), T // 4)], DH.at[pl.ds(k * (T // 4), T // 4)], prev)

    hidden_copy = remote("hid", X.at[1], HID, prev)
    started.append(hidden_copy)

    def forward_one():
        attention(1, 1, False, 0)

        def out_piece(j, carry):
            X[1, :, cols(j)] = (X[1, :, cols(j)].astype(F32) + dot(ATTN[...], Wp[j])).astype(BF16)
            return carry

        lax.fori_loop(0, 8, out_piece, 0)
        hidden_copy.start()

    attention(2, 2, True, T)
    pl.when(odd == 0)(forward_one)
    loads["sg"].wait()
    loads["sq"].wait()
    loads["sp"].wait()

    for k in range(4):
        arrived(f"dh{k}", DH.at[pl.ds(k * (T // 4), T // 4)])

    DACC[...] = jnp.zeros_like(DACC)

    def d_att_two(j, carry):
        DACC[...] += dot_nt(DH[:, cols(j)], Wp[j])
        return carry

    lax.fori_loop(0, 8, d_att_two, 0)
    DATT[...] = DACC[...].astype(BF16)
    attention_back(2, 1)

    def is_own(j):
        return jnp.where(j == own, 1.0, 0.0)

    def grad_qkv(j):
        d_normed = dot_nt(DP[1], Wq[j, 0:C, :])
        xi = XE[:, cols(j)].astype(F32) * wide(INV[2])
        gg = GG[j][0:1, :] + jnp.sum(d_normed * xi, axis=0, keepdims=True)
        Gq[j, C : C + PAD, 0:C] = (jnp.broadcast_to(gg, (PAD, C)) + is_own(j) * SG[...]).astype(BF16)
        block = (xi * gain_row(j)).astype(BF16)
        terms = dot_tn(NS[j], DP[0]) + dot_tn(block, DP[1])
        Gq[j, 0:C, :] = (terms + is_own(j) * SQ[...]).astype(BF16)

    def grad_proj(j):
        terms = dot(ATT_T[:, 0:T], COT[:, cols(j)]) + dot(ATT_T[:, T : 2 * T], DH[:, cols(j)])
        Gp[j] = (terms + is_own(j) * SP[...]).astype(BF16)

    def each(count, work):
        def step(k, carry):
            work(k)
            return carry

        lax.fori_loop(0, count, step, 0)

    def add_q(j, slots, first=0, last=C + PAD):
        def work(k):
            rows = pl.ds(pl.multiple_of(first + k * QR, 16), QR)
            v = Gq[j, rows, :].astype(F32)
            for s in slots:
                v = v + RQ[s, rows, :].astype(F32)
            Gq[j, rows, :] = v.astype(BF16)

        each((last - first) // QR, work)

    def add_p(j, base, size, parts):
        def work(k):
            off = pl.multiple_of(k * 16, 16)
            v = Gp[j, pl.ds(base + off, 16), :].astype(F32)
            for ref in parts:
                v = v + ref[pl.ds(off, 16), :].astype(F32)
            Gp[j, pl.ds(base + off, 16), :] = v.astype(BF16)

        each(size // 16, work)

    result_copy = remote("res", HID, out_h, following)
    started.append(result_copy)

    def forward_two():
        arrived("hid", HID)
        project_all(read_h, 3, 2)
        attention(2, 3, False, 0)

        def result_piece(j, carry):
            HID[:, cols(j)] = (HID[:, cols(j)].astype(F32) + dot(ATTN[...], Wp[j])).astype(BF16)
            return carry

        lax.fori_loop(0, 8, result_piece, 0)
        result_copy.start()

    each(2, lambda k: grad_qkv(at(z + k, x + 2)))

    @pl.when(odd == 0)
    def _():
        pl.semaphore_wait(turn, 1)

    send_both("m1R", Gq.at[jF], RQ.at[0], right)
    send_both("m1L", Gq.at[ozF], RQ.at[1], left)
    each(2, lambda k: grad_qkv(at(z + k, x + 1 + 2 * k)))
    each(4, lambda k: grad_proj(at(z_send, k)))
    for q, off in enumerate((2, 1, 3, 0)):
        send(f"z{q}", Gp.at[at(z_send, x + off)], RPZ.at[q], across)
    for k in range(2):
        arrived_part("m1R", k, RQ.at[0])
        add_q(jR, (0,), *spans[k])
        send_part("m3R", k, Gq.at[jR], RQ.at[4], right)
        arrived_part("m1L", k, RQ.at[1])
        add_q(ozL, (1,), *spans[k])
        send_part("m3L", k, Gq.at[ozL], RQ.at[5], left)
        if k == 0:
            each(2, lambda k: grad_qkv(at(z + 1 + k, x + 1 + 2 * k)))
    for k in range(2):
        send_part("m2R", k, Gq.at[ozR], RQ.at[2], right)
        send_part("m2L", k, Gq.at[jL], RQ.at[3], left)

    @pl.when(odd == 1)
    def _():
        pl.semaphore_signal(turn, inc=1, device_id=prev, device_id_type=MESH)

    pl.when(odd == 1)(forward_two)
    pl.when(odd == 1)(forward_one)
    each(2, lambda k: grad_qkv(at(z + k, x)))
    each(4, lambda k: grad_proj(at(z_keep, k)))
    pl.when(odd == 0)(forward_two)

    kF, kR, kL, kO = (at(z_keep, x + off) for off in (2, 1, 3, 0))
    top, low = pl.ds(0, H2), pl.ds(H2, H2)
    arrived("z0", RPZ.at[0])
    add_p(kF, 0, A, (RPZ.at[0],))
    send("p1R", Gp.at[kF, top], RPX.at[0], right)
    send("p1L", Gp.at[kF, low], RPX.at[1], left)
    arrived("z1", RPZ.at[1])
    add_p(kR, 0, A, (RPZ.at[1],))
    send("p2R", Gp.at[kR, low], RPX.at[2], right)
    arrived("z2", RPZ.at[2])
    add_p(kL, 0, A, (RPZ.at[2],))
    send("p2L", Gp.at[kL, top], RPX.at[3], left)
    j_send, j_keep = at(z_send, x), at(z_keep, x)
    for k in range(2):
        arrived_part("m2R", k, RQ.at[2])
        arrived_part("m2L", k, RQ.at[3])
        arrived_part("m3R", k, RQ.at[4])
        arrived_part("m3L", k, RQ.at[5])
        add_q(j_send, (2 + odd, 5 - odd), *spans[k])
        send_part("mZ", k, Gq.at[j_send], RQ.at[6], across)
    arrived("p1R", RPX.at[0])
    add_p(kR, 0, H2, (RPX.at[0],))
    send("p3R", Gp.at[kR, top], RPX.at[4], right)
    arrived("p1L", RPX.at[1])
    add_p(kL, H2, H2, (RPX.at[1],))
    send("p3L", Gp.at[kL, low], RPX.at[5], left)
    add_q(j_keep, (3 - odd, 4 + odd))
    arrived("z3", RPZ.at[3])
    arrived("p2R", RPX.at[2])
    arrived("p2L", RPX.at[3])
    arrived("p3R", RPX.at[4])
    arrived("p3L", RPX.at[5])
    add_p(kO, 0, H2, (RPZ.at[3, top], RPX.at[4], RPX.at[3]))
    add_p(kO, H2, H2, (RPZ.at[3, low], RPX.at[2], RPX.at[5]))
    send("fp", Gp.at[kO], out_p, following)
    for k in range(2):
        arrived_part("mZ", k, RQ.at[6])
        add_q(j_keep, (6,), *spans[k])
        send_part("fq", k, Gq.at[j_keep], out_q, following)

    arrived("res", out_h)
    arrived("fp", out_p)
    arrived_both("fq", out_q)
    for copy in started:
        copy.wait_send()


def widen(hidden_ref, q_ref, g_ref, p_ref, out_h, out_g, out_q, out_p):
    out_h[...] = hidden_ref[...]
    out_g[...] = g_ref[...].astype(F32)[0:1, : out_g.shape[1]]
    out_q[...] = q_ref[...].astype(F32)
    out_p[...] = p_ref[...].astype(F32)


def body(
    n_blk, x_forward, seg_forward, x_saved, x_earlier, cotangent, seg_backward,
    gain, qkv, proj, sum_gain, sum_qkv, sum_proj,
):
    T, D = x_forward.shape
    C, Q = qkv.shape[1:]
    A = proj.shape[1]
    HD = A // HEADS
    anywhere = pl.BlockSpec(memory_space=pl.ANY)
    V = pltpu.VMEM
    scratch = [
        V((8, C + PAD, Q), BF16), V((8, A, C), BF16), V((8, C + PAD, Q), BF16), V((8, A, C), BF16),
        V((7, C + PAD, Q), BF16), V((4, A, C), BF16), V((6, A // 2, C), BF16),
        V((2, T, D), BF16), V((T, D), BF16), V((T, D), BF16), V((T, D), BF16), V((T, D), BF16),
        V((8, T, C), F32), V((8, T, C), BF16), V((3, T, Q), F32), V((3, T, Q), BF16),
        V((T, A), BF16), V((A, 2 * T), BF16), V((HEADS, T, T), F32), V((2, T, Q), BF16),
        V((T, A), BF16), V((T, A), F32), V((4, T, T), F32), V((T, HD), F32), V((T, HD), F32),
        V((4, T, 128), F32), V((T, 128), F32), V((8, 8, C), F32), V((2, 1, T), jnp.int32),
        V((2, 2, 8, T), F32), V((1, C), BF16), V((1, C), F32), V((C, Q), F32), V((A, C), F32),
        pltpu.SemaphoreType.REGULAR, pltpu.SemaphoreType.REGULAR,
        pltpu.SemaphoreType.DMA((len(MESSAGES),)),
        pltpu.SemaphoreType.DMA((len(MESSAGES),)),
        pltpu.SemaphoreType.DMA((len(LOADS),)),
    ]
    hidden, new_q, new_p = pl.pallas_call(
        functools.partial(kernel, n_blk),
        out_shape=(
            jax.ShapeDtypeStruct((T, D), BF16),
            jax.ShapeDtypeStruct((C + PAD, Q), BF16),
            jax.ShapeDtypeStruct((A, C), BF16),
        ),
        in_specs=[anywhere] * 12,
        out_specs=(anywhere,) * 3,
        scratch_shapes=scratch,
        compiler_params=pltpu.CompilerParams(
            collective_id=0, has_side_effects=True, vmem_limit_bytes=VMEM_LIMIT
        ),
        name="two_steps",
    )(
        x_forward, x_saved, x_earlier, cotangent, seg_forward, seg_backward, qkv[0], gain, proj[0],
        sum_gain, sum_qkv[0], sum_proj[0],
    )
    n = 4
    hidden, new_g, new_q, new_p = pl.pallas_call(
        widen,
        grid=(n,),
        out_shape=(
            jax.ShapeDtypeStruct((T, D), BF16),
            jax.ShapeDtypeStruct((1, C), F32),
            jax.ShapeDtypeStruct((C, Q), F32),
            jax.ShapeDtypeStruct((A, C), F32),
        ),
        in_specs=[
            pl.BlockSpec((T // n, D), lambda i: (i, 0)),
            pl.BlockSpec((C // n, Q), lambda i: (i, 0)),
            pl.BlockSpec((PAD, Q), lambda i: (C // PAD, 0)),
            pl.BlockSpec((A // n, C), lambda i: (i, 0)),
        ],
        out_specs=(
            pl.BlockSpec((T // n, D), lambda i: (i, 0)),
            pl.BlockSpec((1, C), lambda i: (0, 0)),
            pl.BlockSpec((C // n, Q), lambda i: (i, 0)),
            pl.BlockSpec((A // n, C), lambda i: (i, 0)),
        ),
        name="widen",
    )(hidden, new_q, new_q, new_p)
    return hidden, new_g, new_q[None], new_p[None]


def solution(mesh):
    rows, layer = P(("blk", "fsdp"), None), P("blk", "fsdp")
    q_spec, p_spec = P("blk", "fsdp", None), P("blk", None, "fsdp")
    return jax.shard_map(
        functools.partial(body, mesh.shape["blk"]),
        mesh=mesh,
        in_specs=(rows,) * 6 + (layer, q_spec, p_spec) * 2,
        out_specs=(rows, layer, q_spec, p_spec),
        check_vma=False,
    )
```

```python
import functools

import jax
import jax.numpy as jnp
from jax import lax
from jax.experimental import pallas as pl
from jax.experimental.pallas import tpu as pltpu
from jax.sharding import PartitionSpec as P

HEADS = 4
PAD = 16
VMEM_LIMIT = 64 * 1024 * 1024 - 256 * 1024
MESH = pl.DeviceIdType.MESH
F32, BF16 = jnp.float32, jnp.bfloat16

MESSAGES = (
    "xe", "seg", "pR", "pL", "pZ0", "pZ1", "pZ2", "pZ3", "pRf", "pLf", "dh0", "dh1", "dh2", "dh3",
    "hid", "res", "z0", "z1", "z2", "z3", "p1R", "p1L", "p2R", "p2L", "p3R", "p3L", "fp", "qZ_0",
    "qZ_1", "qR_0", "qR_1", "qL_0", "qL_1", "cR_0", "cR_1", "cL_0", "cL_1", "eR_0", "eR_1", "eL_0",
    "eL_1", "m1R_0", "m1R_1", "m1L_0", "m1L_1", "m2R_0", "m2R_1", "m2L_0", "m2L_1", "m3R_0",
    "m3R_1", "m3L_0", "m3L_1", "mZ_0", "mZ_1", "fq_0", "fq_1",
)
LOADS = (
    "wq", "wg", "wp", "xs", "xf", "cot", "sf", "sb", "sg", "sq", "sp",
)


def dot(a, b):
    return lax.dot_general(a, b, (((1,), (0,)), ((), ())), preferred_element_type=F32)


def dot_nt(a, b):
    return lax.dot_general(a, b, (((1,), (1,)), ((), ())), preferred_element_type=F32)


def dot_tn(a, b):
    return lax.dot_general(a, b, (((0,), (0,)), ((), ())), preferred_element_type=F32)


def kernel(
    n_blk, xf_in, xs_in, xe_in, cot_in, sf_in, sb_in, qkv_in, gain_in, proj_in, sg_in, sq_in, sp_in,
    out_h, out_q, out_p,
    Wq, Wp, Gq, Gp, RQ, RPZ, RPX, X, XE, COT, HID, DH, DN, NS, ACC, PR, ATTN, ATT_T, PROBS, DP, DATT, DACC,
    MASK, GK, GV, INV, CO, GG, SEGI, SEG, GN, SG, SQ, SP, go, turn, send_sem, recv_sem, load_sem,
):
    T, D = COT.shape
    C = Wq.shape[1] - PAD
    Q = Wq.shape[2]
    A = Wp.shape[1]
    HD = A // HEADS
    H2 = A // 2
    scale = HD ** (-0.5)
    QR = 48 if (C + PAD) % 48 == 0 else 16

    b, f = lax.axis_index("blk"), lax.axis_index("fsdp")
    z, x = lax.div(f, 4), lax.rem(f, 4)
    odd = lax.rem(b, 2)

    def at(zz, xx):
        return lax.rem(zz, 2) * 4 + lax.rem(xx, 4)

    own, jL, jR, jF = f, at(z, x + 3), at(z, x + 1), at(z, x + 2)
    oz, ozL, ozR, ozF = at(z + 1, x), at(z + 1, x + 3), at(z + 1, x + 1), at(z + 1, x + 2)
    right, left, across = (b, jR), (b, jL), (b, oz)
    prev = (lax.rem(b + n_blk - 1, n_blk), lax.rem(f + 4 * (1 - odd), 8))
    following = (lax.rem(b + 1, n_blk), lax.rem(f + 4 * odd, 8))
    z_keep, z_send = z + odd, z + 1 + odd

    started = []

    def remote(name, src, dst, device):
        k = MESSAGES.index(name)
        return pltpu.make_async_remote_copy(
            src_ref=src, dst_ref=dst, send_sem=send_sem.at[k], recv_sem=recv_sem.at[k],
            device_id=device, device_id_type=MESH,
        )

    def send(name, src, dst, device):
        copy = remote(name, src, dst, device)
        copy.start()
        started.append(copy)

    def arrived(name, dst):
        remote(name, dst, dst, right).wait_recv()

    cut = (C + PAD) // QR // 2 * QR
    spans = ((0, cut), (cut, C + PAD))
    parts = (pl.ds(0, cut), pl.ds(cut, C + PAD - cut))

    def send_part(name, k, src, dst, device):
        send(f"{name}_{k}", src.at[parts[k]], dst.at[parts[k]], device)

    def send_both(name, src, dst, device):
        for k in range(2):
            send_part(name, k, src, dst, device)

    def arrived_part(name, k, dst):
        arrived(f"{name}_{k}", dst.at[parts[k]])

    def arrived_both(name, dst):
        for k in range(2):
            arrived_part(name, k, dst)

    loads = {}

    def load(name, src, dst):
        loads[name] = pltpu.make_async_copy(src, dst, load_sem.at[LOADS.index(name)])
        loads[name].start()

    def cols(j):
        return pl.ds(pl.multiple_of(j * C, C), C)

    def wide(v):
        return jnp.concatenate([v] * (C // v.shape[1]), axis=1) if C > v.shape[1] else v

    def folded(v):
        total = v[:, 0:128]
        for k in range(1, v.shape[1] // 128):
            total = total + v[:, k * 128 : (k + 1) * 128]
        return total

    load("wp", proj_in, Wp.at[own])
    load("wq", qkv_in, Wq.at[own, pl.ds(0, C)])
    load("wg", gain_in, GN)
    load("sf", sf_in, SEGI.at[0])
    load("sb", sb_in, SEGI.at[1])
    load("xs", xs_in, X.at[0])
    load("xf", xf_in, X.at[1])
    load("cot", cot_in, COT)
    load("sg", sg_in, SG)
    load("sq", sq_in, SQ)
    load("sp", sp_in, SP)
    barrier = pltpu.get_barrier_semaphore()
    for device in (right, left, across, prev, following):
        pl.semaphore_signal(barrier, inc=1, device_id=device, device_id_type=MESH)
    loads["wg"].wait()
    loads["sf"].wait()
    loads["sb"].wait()
    SEG[0, 0] = jnp.broadcast_to(SEGI[0].astype(F32), (8, T))
    SEG[0, 1] = jnp.broadcast_to(SEGI[1].astype(F32), (8, T))
    loads["wq"].wait()
    Wq[own, C : C + PAD, 0:C] = jnp.broadcast_to(GN[...].astype(F32), (PAD, C)).astype(BF16)
    Wq[own, C : C + PAD, C:Q] = jnp.zeros((PAD, Q - C), BF16)
    loads["wp"].wait()
    pl.semaphore_wait(barrier, 5)

    send("xe", xe_in, XE, prev)
    send("seg", SEG.at[0], SEG.at[1], prev)

    def gather_starts():
        copies = [
            remote("pR", Wp.at[own], Wp.at[own], right),
            remote("pL", Wp.at[own], Wp.at[own], left),
        ]
        for name, device in (("qZ", across), ("qR", right)):
            for k in range(2):
                piece = Wq.at[own, parts[k]]
                copies.append(remote(f"{name}_{k}", piece, piece, device))
        return copies

    first_copies = gather_starts()
    started.extend(first_copies)

    @pl.when(odd == 0)
    def _():
        for copy in first_copies:
            copy.start()

    def make_mask(place, kind, slot):
        row = jnp.broadcast_to(SEG[place, kind, 0:1, :], (T, T))
        col = row.T
        i = lax.broadcasted_iota(jnp.int32, (T, T), 0)
        j = lax.broadcasted_iota(jnp.int32, (T, T), 1)
        MASK[slot] = jnp.where((j <= i) & (row == col), 1.0, 0.0)

    def rms(read, slot):
        def step(j, total):
            v = read(cols(j)).astype(F32)
            return total + folded(v * v)

        total = lax.fori_loop(0, 8, step, jnp.zeros((T, 128), F32))
        inv = lax.rsqrt(jnp.sum(total, axis=1, keepdims=True) * (1.0 / D) + 1e-05)
        INV[slot] = jnp.broadcast_to(inv, (T, 128))

    def gain_row(j):
        return Wq[j, C : C + PAD, 0:C][0:1, :].astype(F32)

    def normed(read, slot, j):
        v = read(cols(j)).astype(F32)
        return (v * wide(INV[slot]) * gain_row(j)).astype(BF16)

    def read_s(c):
        return X[0, :, c]

    def read_f(c):
        return X[1, :, c]

    def read_e(c):
        return XE[:, c]

    def read_h(c):
        return HID[:, c]

    def project_piece(j):
        for i, read in ((0, read_s), (1, read_f), (2, read_e)):
            block = normed(read, i, j)
            if i == 0:
                NS[j] = block
            ACC[i] += dot(block, Wq[j, 0:C, :])

    def project_all(read, slot, dst):
        rms(read, slot)
        ACC[0] = jnp.zeros((T, Q), F32)

        def step(j, carry):
            ACC[0] += dot(normed(read, slot, j), Wq[j, 0:C, :])
            return carry

        lax.fori_loop(0, 8, step, 0)
        PR[dst] = ACC[0].astype(BF16)

    def head(h):
        return slice(h * HD, (h + 1) * HD)

    def attention(src, mask_slot, probs, t_off):
        def step(h, carry):
            allowed = MASK[mask_slot] > 0.5
            s = dot_nt(PR[src, :, head(h)], PR[src, :, A : A + HD]) * scale
            s = jnp.where(allowed, s, -1e30)
            e = jnp.where(allowed, jnp.exp(s - jnp.max(s, axis=1, keepdims=True)), 0.0)
            p = e / jnp.sum(e, axis=1, keepdims=True)
            if probs:
                PROBS[h] = p
            out = dot(p.astype(BF16), PR[src, :, A + HD : A + 2 * HD])
            if probs:
                ATT_T[head(h), t_off : t_off + T] = out.T.astype(BF16)
            else:
                ATTN[:, head(h)] = out.astype(BF16)
            return carry

        for h in range(HEADS):
            step(h, 0)

    def attention_back(src, dst):
        GK[...] = jnp.zeros_like(GK)
        GV[...] = jnp.zeros_like(GV)

        def step(h, carry):
            d_head = DATT[:, head(h)]
            p = PROBS[h]
            dp = dot_nt(d_head, PR[src, :, A + HD : A + 2 * HD])
            inner = jnp.sum(dp * p, axis=1, keepdims=True)
            ds = (p * (dp - inner) * scale).astype(BF16)
            DP[dst, :, head(h)] = dot(ds, PR[src, :, A : A + HD]).astype(BF16)
            GK[...] += dot_tn(ds, PR[src, :, head(h)])
            GV[...] += dot_tn(p.astype(BF16), d_head)
            return carry

        for h in range(HEADS):
            step(h, 0)
        DP[dst, :, A : A + HD] = GK[...].astype(BF16)
        DP[dst, :, A + HD : A + 2 * HD] = GV[...].astype(BF16)

    def d_att_piece(j):
        DACC[...] += dot_nt(COT[:, cols(j)], Wp[j])

    make_mask(0, 1, 0)
    make_mask(0, 0, 1)
    for j in range(8):
        Gq[j, C : C + PAD, :] = jnp.zeros((PAD, Q), BF16)
    ACC[...] = jnp.zeros_like(ACC)
    DACC[...] = jnp.zeros_like(DACC)
    loads["xs"].wait()
    rms(read_s, 0)
    loads["xf"].wait()
    rms(read_f, 1)
    loads["cot"].wait()
    arrived("seg", SEG.at[1])
    make_mask(1, 1, 2)
    make_mask(1, 0, 3)

    @pl.when(odd == 1)
    def _():
        pl.semaphore_wait(go, 1)
        for copy in first_copies:
            copy.start()

    arrived_part("qZ", 0, Wq.at[oz])
    send_part("cL", 0, Wq.at[oz], Wq.at[oz], left)
    send_part("cR", 0, Wq.at[oz], Wq.at[oz], right)
    send("pZ0", Wp.at[own], Wp.at[own], across)
    arrived("pR", Wp.at[jL])
    send("pRf", Wp.at[jL, pl.ds(0, H2)], Wp.at[jL, pl.ds(0, H2)], right)
    send("pZ1", Wp.at[jL], Wp.at[jL], across)
    arrived("pL", Wp.at[jR])
    send("pLf", Wp.at[jR, pl.ds(H2, H2)], Wp.at[jR, pl.ds(H2, H2)], left)
    send("pZ2", Wp.at[jR], Wp.at[jR], across)
    arrived_part("qZ", 1, Wq.at[oz])
    send_part("cL", 1, Wq.at[oz], Wq.at[oz], left)
    send_part("cR", 1, Wq.at[oz], Wq.at[oz], right)
    send_both("qL", Wq.at[own], Wq.at[own], left)
    arrived_part("qR", 0, Wq.at[jL])
    send_part("eR", 0, Wq.at[jL], Wq.at[jL], right)
    arrived("xe", XE)
    rms(read_e, 2)
    project_piece(own)
    arrived_part("qR", 1, Wq.at[jL])
    send_part("eR", 1, Wq.at[jL], Wq.at[jL], right)
    arrived("pRf", Wp.at[jF, pl.ds(0, H2)])
    arrived("pLf", Wp.at[jF, pl.ds(H2, H2)])
    send("pZ3", Wp.at[jF], Wp.at[jF], across)
    project_piece(oz)
    project_piece(jL)
    arrived_part("cL", 0, Wq.at[ozR])
    send_part("eL", 0, Wq.at[ozR], Wq.at[ozR], left)
    arrived_both("qL", Wq.at[jR])
    project_piece(jR)
    arrived_part("cL", 1, Wq.at[ozR])
    send_part("eL", 1, Wq.at[ozR], Wq.at[ozR], left)

    @pl.when(odd == 0)
    def _():
        pl.semaphore_signal(go, inc=1, device_id=following, device_id_type=MESH)

    d_att_piece(own)
    d_att_piece(jL)
    d_att_piece(jR)
    d_att_piece(jF)
    project_piece(ozR)
    arrived_both("cR", Wq.at[ozL])
    project_piece(ozL)
    arrived("pZ0", Wp.at[oz])
    d_att_piece(oz)
    arrived("pZ1", Wp.at[ozL])
    d_att_piece(ozL)
    arrived("pZ2", Wp.at[ozR])
    d_att_piece(ozR)
    arrived_both("eR", Wq.at[jF])
    project_piece(jF)
    arrived_both("eL", Wq.at[ozF])
    project_piece(ozF)
    PR[0] = ACC[0].astype(BF16)
    PR[1] = ACC[1].astype(BF16)
    PR[2] = ACC[2].astype(BF16)
    attention(0, 0, True, 0)
    arrived("pZ3", Wp.at[ozF])
    d_att_piece(ozF)
    DATT[...] = DACC[...].astype(BF16)

    attention_back(0, 0)

    def scaled_piece(j, total):
        d_normed = dot_nt(DP[0], Wq[j, 0:C, :])
        v = X[0, :, cols(j)].astype(F32)
        GG[j] = jnp.broadcast_to(jnp.sum(d_normed * (v * wide(INV[0])), axis=0, keepdims=True), (8, C))
        scaled = d_normed * gain_row(j)
        DN[j] = scaled
        return total + folded(scaled * v)

    total = lax.fori_loop(0, 8, scaled_piece, jnp.zeros((T, 128), F32))
    inv = INV[0]
    CO[...] = inv * inv * inv * (jnp.sum(total, axis=1, keepdims=True) * (1.0 / D))
    dx_copies = []
    for k in range(4):
        rows = pl.ds(k * (T // 4), T // 4)
        dx_copies.append(remote(f"dh{k}", X.at[0, rows], DH.at[rows], prev))
    started.extend(dx_copies)

    def send_dx():
        for k in range(4):
            rows = slice(k * (T // 4), (k + 1) * (T // 4))

            def dx_piece(j, carry):
                v = X[0, rows, cols(j)].astype(F32)
                d_wide = wide(INV[0, rows, :]) * DN[j, rows, :] - v * wide(CO[rows, :])
                X[0, rows, cols(j)] = (COT[rows, cols(j)].astype(F32) + d_wide).astype(BF16)
                return carry

            lax.fori_loop(0, 8, dx_piece, 0)
            dx_copies[k].start()

    pl.when(odd == 0)(send_dx)

    hidden_copy = remote("hid", X.at[1], HID, prev)
    started.append(hidden_copy)

    def forward_one():
        attention(1, 1, False, 0)

        def out_piece(j, carry):
            X[1, :, cols(j)] = (X[1, :, cols(j)].astype(F32) + dot(ATTN[...], Wp[j])).astype(BF16)
            return carry

        lax.fori_loop(0, 8, out_piece, 0)
        hidden_copy.start()

    attention(2, 2, True, T)
    pl.when(odd == 0)(forward_one)
    loads["sg"].wait()
    loads["sq"].wait()
    loads["sp"].wait()

    for k in range(4):
        arrived(f"dh{k}", DH.at[pl.ds(k * (T // 4), T // 4)])

    DACC[...] = jnp.zeros_like(DACC)

    def d_att_two(j, carry):
        DACC[...] += dot_nt(DH[:, cols(j)], Wp[j])
        return carry

    lax.fori_loop(0, 8, d_att_two, 0)
    DATT[...] = DACC[...].astype(BF16)
    attention_back(2, 1)

    def is_own(j):
        return jnp.where(j == own, 1.0, 0.0)

    def grad_qkv(j):
        d_normed = dot_nt(DP[1], Wq[j, 0:C, :])
        xi = XE[:, cols(j)].astype(F32) * wide(INV[2])
        gg = GG[j][0:1, :] + jnp.sum(d_normed * xi, axis=0, keepdims=True)
        Gq[j, C : C + PAD, 0:C] = (jnp.broadcast_to(gg, (PAD, C)) + is_own(j) * SG[...]).astype(BF16)
        block = (xi * gain_row(j)).astype(BF16)
        terms = dot_tn(NS[j], DP[0]) + dot_tn(block, DP[1])
        Gq[j, 0:C, :] = (terms + is_own(j) * SQ[...]).astype(BF16)

    def grad_proj(j):
        terms = dot(ATT_T[:, 0:T], COT[:, cols(j)]) + dot(ATT_T[:, T : 2 * T], DH[:, cols(j)])
        Gp[j] = (terms + is_own(j) * SP[...]).astype(BF16)

    def each(count, work):
        def step(k, carry):
            work(k)
            return carry

        lax.fori_loop(0, count, step, 0)

    def add_q(j, slots, first=0, last=C + PAD):
        def work(k):
            rows = pl.ds(pl.multiple_of(first + k * QR, 16), QR)
            v = Gq[j, rows, :].astype(F32)
            for s in slots:
                v = v + RQ[s, rows, :].astype(F32)
            Gq[j, rows, :] = v.astype(BF16)

        each((last - first) // QR, work)

    def add_p(j, base, size, parts):
        def work(k):
            off = pl.multiple_of(k * 16, 16)
            v = Gp[j, pl.ds(base + off, 16), :].astype(F32)
            for ref in parts:
                v = v + ref[pl.ds(off, 16), :].astype(F32)
            Gp[j, pl.ds(base + off, 16), :] = v.astype(BF16)

        each(size // 16, work)

    result_copy = remote("res", HID, out_h, following)
    started.append(result_copy)

    def forward_two():
        arrived("hid", HID)
        project_all(read_h, 3, 2)
        attention(2, 3, False, 0)

        def result_piece(j, carry):
            HID[:, cols(j)] = (HID[:, cols(j)].astype(F32) + dot(ATTN[...], Wp[j])).astype(BF16)
            return carry

        lax.fori_loop(0, 8, result_piece, 0)
        result_copy.start()

    each(2, lambda k: grad_qkv(at(z + k, x + 2)))

    @pl.when(odd == 0)
    def _():
        pl.semaphore_wait(turn, 1)

    send_both("m1R", Gq.at[jF], RQ.at[0], right)
    send_both("m1L", Gq.at[ozF], RQ.at[1], left)
    pl.when(odd == 1)(send_dx)
    each(2, lambda k: grad_qkv(at(z + k, x + 1 + 2 * k)))
    each(4, lambda k: grad_proj(at(z_send, k)))
    for q, off in enumerate((2, 1, 3, 0)):
        send(f"z{q}", Gp.at[at(z_send, x + off)], RPZ.at[q], across)
    for k in range(2):
        arrived_part("m1R", k, RQ.at[0])
        add_q(jR, (0,), *spans[k])
        send_part("m3R", k, Gq.at[jR], RQ.at[4], right)
        arrived_part("m1L", k, RQ.at[1])
        add_q(ozL, (1,), *spans[k])
        send_part("m3L", k, Gq.at[ozL], RQ.at[5], left)
        if k == 0:
            each(2, lambda k: grad_qkv(at(z + 1 + k, x + 1 + 2 * k)))
    for k in range(2):
        send_part("m2R", k, Gq.at[ozR], RQ.at[2], right)
        send_part("m2L", k, Gq.at[jL], RQ.at[3], left)

    @pl.when(odd == 1)
    def _():
        pl.semaphore_signal(turn, inc=1, device_id=prev, device_id_type=MESH)

    pl.when(odd == 1)(forward_two)
    pl.when(odd == 1)(forward_one)
    each(2, lambda k: grad_qkv(at(z + k, x)))
    each(4, lambda k: grad_proj(at(z_keep, k)))
    pl.when(odd == 0)(forward_two)

    kF, kR, kL, kO = (at(z_keep, x + off) for off in (2, 1, 3, 0))
    top, low = pl.ds(0, H2), pl.ds(H2, H2)
    arrived("z0", RPZ.at[0])
    add_p(kF, 0, A, (RPZ.at[0],))
    send("p1R", Gp.at[kF, top], RPX.at[0], right)
    send("p1L", Gp.at[kF, low], RPX.at[1], left)
    arrived("z1", RPZ.at[1])
    add_p(kR, 0, A, (RPZ.at[1],))
    send("p2R", Gp.at[kR, low], RPX.at[2], right)
    arrived("z2", RPZ.at[2])
    add_p(kL, 0, A, (RPZ.at[2],))
    send("p2L", Gp.at[kL, top], RPX.at[3], left)
    j_send, j_keep = at(z_send, x), at(z_keep, x)
    for k in range(2):
        arrived_part("m2R", k, RQ.at[2])
        arrived_part("m2L", k, RQ.at[3])
        arrived_part("m3R", k, RQ.at[4])
        arrived_part("m3L", k, RQ.at[5])
        add_q(j_send, (2 + odd, 5 - odd), *spans[k])
        send_part("mZ", k, Gq.at[j_send], RQ.at[6], across)
    arrived("p1R", RPX.at[0])
    add_p(kR, 0, H2, (RPX.at[0],))
    send("p3R", Gp.at[kR, top], RPX.at[4], right)
    arrived("p1L", RPX.at[1])
    add_p(kL, H2, H2, (RPX.at[1],))
    send("p3L", Gp.at[kL, low], RPX.at[5], left)
    add_q(j_keep, (3 - odd, 4 + odd))
    arrived("z3", RPZ.at[3])
    arrived("p2R", RPX.at[2])
    arrived("p2L", RPX.at[3])
    arrived("p3R", RPX.at[4])
    arrived("p3L", RPX.at[5])
    add_p(kO, 0, H2, (RPZ.at[3, top], RPX.at[4], RPX.at[3]))
    add_p(kO, H2, H2, (RPZ.at[3, low], RPX.at[2], RPX.at[5]))
    send("fp", Gp.at[kO], out_p, following)
    for k in range(2):
        arrived_part("mZ", k, RQ.at[6])
        add_q(j_keep, (6,), *spans[k])
        send_part("fq", k, Gq.at[j_keep], out_q, following)

    arrived("res", out_h)
    arrived("fp", out_p)
    arrived_both("fq", out_q)
    for copy in started:
        copy.wait_send()


def widen(hidden_ref, q_ref, g_ref, p_ref, out_h, out_g, out_q, out_p):
    out_h[...] = hidden_ref[...]
    out_g[...] = g_ref[...].astype(F32)[0:1, : out_g.shape[1]]
    out_q[...] = q_ref[...].astype(F32)
    out_p[...] = p_ref[...].astype(F32)


def body(
    n_blk, x_forward, seg_forward, x_saved, x_earlier, cotangent, seg_backward,
    gain, qkv, proj, sum_gain, sum_qkv, sum_proj,
):
    T, D = x_forward.shape
    C, Q = qkv.shape[1:]
    A = proj.shape[1]
    HD = A // HEADS
    anywhere = pl.BlockSpec(memory_space=pl.ANY)
    V = pltpu.VMEM
    scratch = [
        V((8, C + PAD, Q), BF16), V((8, A, C), BF16), V((8, C + PAD, Q), BF16), V((8, A, C), BF16),
        V((7, C + PAD, Q), BF16), V((4, A, C), BF16), V((6, A // 2, C), BF16),
        V((2, T, D), BF16), V((T, D), BF16), V((T, D), BF16), V((T, D), BF16), V((T, D), BF16),
        V((8, T, C), F32), V((8, T, C), BF16), V((3, T, Q), F32), V((3, T, Q), BF16),
        V((T, A), BF16), V((A, 2 * T), BF16), V((HEADS, T, T), F32), V((2, T, Q), BF16),
        V((T, A), BF16), V((T, A), F32), V((4, T, T), F32), V((T, HD), F32), V((T, HD), F32),
        V((4, T, 128), F32), V((T, 128), F32), V((8, 8, C), F32), V((2, 1, T), jnp.int32),
        V((2, 2, 8, T), F32), V((1, C), BF16), V((1, C), F32), V((C, Q), F32), V((A, C), F32),
        pltpu.SemaphoreType.REGULAR, pltpu.SemaphoreType.REGULAR,
        pltpu.SemaphoreType.DMA((len(MESSAGES),)),
        pltpu.SemaphoreType.DMA((len(MESSAGES),)),
        pltpu.SemaphoreType.DMA((len(LOADS),)),
    ]
    hidden, new_q, new_p = pl.pallas_call(
        functools.partial(kernel, n_blk),
        out_shape=(
            jax.ShapeDtypeStruct((T, D), BF16),
            jax.ShapeDtypeStruct((C + PAD, Q), BF16),
            jax.ShapeDtypeStruct((A, C), BF16),
        ),
        in_specs=[anywhere] * 12,
        out_specs=(anywhere,) * 3,
        scratch_shapes=scratch,
        compiler_params=pltpu.CompilerParams(
            collective_id=0, has_side_effects=True, vmem_limit_bytes=VMEM_LIMIT
        ),
        name="two_steps",
    )(
        x_forward, x_saved, x_earlier, cotangent, seg_forward, seg_backward, qkv[0], gain, proj[0],
        sum_gain, sum_qkv[0], sum_proj[0],
    )
    n = 4
    hidden, new_g, new_q, new_p = pl.pallas_call(
        widen,
        grid=(n,),
        out_shape=(
            jax.ShapeDtypeStruct((T, D), BF16),
            jax.ShapeDtypeStruct((1, C), F32),
            jax.ShapeDtypeStruct((C, Q), F32),
            jax.ShapeDtypeStruct((A, C), F32),
        ),
        in_specs=[
            pl.BlockSpec((T // n, D), lambda i: (i, 0)),
            pl.BlockSpec((C // n, Q), lambda i: (i, 0)),
            pl.BlockSpec((PAD, Q), lambda i: (C // PAD, 0)),
            pl.BlockSpec((A // n, C), lambda i: (i, 0)),
        ],
        out_specs=(
            pl.BlockSpec((T // n, D), lambda i: (i, 0)),
            pl.BlockSpec((1, C), lambda i: (0, 0)),
            pl.BlockSpec((C // n, Q), lambda i: (i, 0)),
            pl.BlockSpec((A // n, C), lambda i: (i, 0)),
        ),
        name="widen",
    )(hidden, new_q, new_q, new_p)
    return hidden, new_g, new_q[None], new_p[None]


def solution(mesh):
    rows, layer = P(("blk", "fsdp"), None), P("blk", "fsdp")
    q_spec, p_spec = P("blk", "fsdp", None), P("blk", None, "fsdp")
    return jax.shard_map(
        functools.partial(body, mesh.shape["blk"]),
        mesh=mesh,
        in_specs=(rows,) * 6 + (layer, q_spec, p_spec) * 2,
        out_specs=(rows, layer, q_spec, p_spec),
        check_vma=False,
    )
```

```python
import functools

import jax
import jax.numpy as jnp
from jax import lax
from jax.experimental import pallas as pl
from jax.experimental.pallas import tpu as pltpu
from jax.sharding import PartitionSpec as P

HEADS = 4
PAD = 16
VMEM_LIMIT = 64 * 1024 * 1024 - 256 * 1024
MESH = pl.DeviceIdType.MESH
F32, BF16 = jnp.float32, jnp.bfloat16

MESSAGES = (
    "xe", "seg", "pR", "pL", "pZ0", "pZ1", "pZ2", "pZ3", "pRf", "pLf", "dh0", "dh1", "dh2", "dh3",
    "hid", "res", "z0", "z1", "z2", "z3", "p1R", "p1L", "p2R", "p2L", "p3R", "p3L", "fp", "qZ_0",
    "qZ_1", "qR_0", "qR_1", "qL_0", "qL_1", "cR_0", "cR_1", "cL_0", "cL_1", "eR_0", "eR_1", "eL_0",
    "eL_1", "m1R_0", "m1R_1", "m1L_0", "m1L_1", "m2R_0", "m2R_1", "m2L_0", "m2L_1", "m3R_0",
    "m3R_1", "m3L_0", "m3L_1", "mZ_0", "mZ_1", "fq_0", "fq_1",
)
LOADS = (
    "wq", "wg", "wp", "xs", "xf", "cot", "sf", "sb", "sg", "sq", "sp",
)


def dot(a, b):
    return lax.dot_general(a, b, (((1,), (0,)), ((), ())), preferred_element_type=F32)


def dot_nt(a, b):
    return lax.dot_general(a, b, (((1,), (1,)), ((), ())), preferred_element_type=F32)


def dot_tn(a, b):
    return lax.dot_general(a, b, (((0,), (0,)), ((), ())), preferred_element_type=F32)


def kernel(
    n_blk, xf_in, xs_in, xe_in, cot_in, sf_in, sb_in, qkv_in, gain_in, proj_in, sg_in, sq_in, sp_in,
    out_h, out_q, out_p,
    Wq, Wp, Gq, Gp, RQ, RPZ, RPX, X, XE, COT, HID, DH, DN, NS, ACC, PR, ATTN, ATT_T, PROBS, DP, DATT, DACC,
    MASK, GK, GV, INV, CO, GG, SEGI, SEG, GN, SG, SQ, SP, go, turn, send_sem, recv_sem, load_sem,
):
    T, D = COT.shape
    C = Wq.shape[1] - PAD
    Q = Wq.shape[2]
    A = Wp.shape[1]
    HD = A // HEADS
    H2 = A // 2
    scale = HD ** (-0.5)
    QR = 48 if (C + PAD) % 48 == 0 else 16

    b, f = lax.axis_index("blk"), lax.axis_index("fsdp")
    z, x = lax.div(f, 4), lax.rem(f, 4)
    odd = lax.rem(b, 2)

    def at(zz, xx):
        return lax.rem(zz, 2) * 4 + lax.rem(xx, 4)

    own, jL, jR, jF = f, at(z, x + 3), at(z, x + 1), at(z, x + 2)
    oz, ozL, ozR, ozF = at(z + 1, x), at(z + 1, x + 3), at(z + 1, x + 1), at(z + 1, x + 2)
    right, left, across = (b, jR), (b, jL), (b, oz)
    prev = (lax.rem(b + n_blk - 1, n_blk), lax.rem(f + 4 * (1 - odd), 8))
    following = (lax.rem(b + 1, n_blk), lax.rem(f + 4 * odd, 8))
    z_keep, z_send = z + odd, z + 1 + odd

    started = []

    def remote(name, src, dst, device):
        k = MESSAGES.index(name)
        return pltpu.make_async_remote_copy(
            src_ref=src, dst_ref=dst, send_sem=send_sem.at[k], recv_sem=recv_sem.at[k],
            device_id=device, device_id_type=MESH,
        )

    def send(name, src, dst, device):
        copy = remote(name, src, dst, device)
        copy.start()
        started.append(copy)

    def arrived(name, dst):
        remote(name, dst, dst, right).wait_recv()

    cut = (C + PAD) // QR // 2 * QR
    spans = ((0, cut), (cut, C + PAD))
    parts = (pl.ds(0, cut), pl.ds(cut, C + PAD - cut))

    def send_part(name, k, src, dst, device):
        send(f"{name}_{k}", src.at[parts[k]], dst.at[parts[k]], device)

    def send_both(name, src, dst, device):
        for k in range(2):
            send_part(name, k, src, dst, device)

    def arrived_part(name, k, dst):
        arrived(f"{name}_{k}", dst.at[parts[k]])

    def arrived_both(name, dst):
        for k in range(2):
            arrived_part(name, k, dst)

    loads = {}

    def load(name, src, dst):
        loads[name] = pltpu.make_async_copy(src, dst, load_sem.at[LOADS.index(name)])
        loads[name].start()

    def cols(j):
        return pl.ds(pl.multiple_of(j * C, C), C)

    def wide(v):
        return jnp.concatenate([v] * (C // v.shape[1]), axis=1) if C > v.shape[1] else v

    def folded(v):
        total = v[:, 0:128]
        for k in range(1, v.shape[1] // 128):
            total = total + v[:, k * 128 : (k + 1) * 128]
        return total

    load("wp", proj_in, Wp.at[own])
    load("wq", qkv_in, Wq.at[own, pl.ds(0, C)])
    load("wg", gain_in, GN)
    load("sf", sf_in, SEGI.at[0])
    load("sb", sb_in, SEGI.at[1])
    load("xs", xs_in, X.at[0])
    load("xf", xf_in, X.at[1])
    load("cot", cot_in, COT)
    load("sg", sg_in, SG)
    load("sq", sq_in, SQ)
    load("sp", sp_in, SP)
    barrier = pltpu.get_barrier_semaphore()
    for device in (right, left, across, prev, following):
        pl.semaphore_signal(barrier, inc=1, device_id=device, device_id_type=MESH)
    loads["wg"].wait()
    loads["sf"].wait()
    loads["sb"].wait()
    SEG[0, 0] = jnp.broadcast_to(SEGI[0].astype(F32), (8, T))
    SEG[0, 1] = jnp.broadcast_to(SEGI[1].astype(F32), (8, T))
    loads["wq"].wait()
    Wq[own, C : C + PAD, 0:C] = jnp.broadcast_to(GN[...].astype(F32), (PAD, C)).astype(BF16)
    Wq[own, C : C + PAD, C:Q] = jnp.zeros((PAD, Q - C), BF16)
    loads["wp"].wait()
    pl.semaphore_wait(barrier, 5)

    send("xe", xe_in, XE, prev)
    send("seg", SEG.at[0], SEG.at[1], prev)

    def gather_starts():
        copies = [
            remote("pR", Wp.at[own], Wp.at[own], right),
            remote("pL", Wp.at[own], Wp.at[own], left),
        ]
        for name, device in (("qZ", across), ("qR", right)):
            for k in range(2):
                piece = Wq.at[own, parts[k]]
                copies.append(remote(f"{name}_{k}", piece, piece, device))
        return copies

    first_copies = gather_starts()
    started.extend(first_copies)

    @pl.when(odd == 0)
    def _():
        for copy in first_copies:
            copy.start()

    def make_mask(place, kind, slot):
        row = jnp.broadcast_to(SEG[place, kind, 0:1, :], (T, T))
        col = row.T
        i = lax.broadcasted_iota(jnp.int32, (T, T), 0)
        j = lax.broadcasted_iota(jnp.int32, (T, T), 1)
        MASK[slot] = jnp.where((j <= i) & (row == col), 1.0, 0.0)

    def rms(read, slot):
        def step(j, total):
            v = read(cols(j)).astype(F32)
            return total + folded(v * v)

        total = lax.fori_loop(0, 8, step, jnp.zeros((T, 128), F32))
        inv = lax.rsqrt(jnp.sum(total, axis=1, keepdims=True) * (1.0 / D) + 1e-05)
        INV[slot] = jnp.broadcast_to(inv, (T, 128))

    def gain_row(j):
        return Wq[j, C : C + PAD, 0:C][0:1, :].astype(F32)

    def normed(read, slot, j):
        v = read(cols(j)).astype(F32)
        return (v * wide(INV[slot]) * gain_row(j)).astype(BF16)

    def read_s(c):
        return X[0, :, c]

    def read_f(c):
        return X[1, :, c]

    def read_e(c):
        return XE[:, c]

    def read_h(c):
        return HID[:, c]

    def project_piece(j):
        for i, read in ((0, read_s), (1, read_f), (2, read_e)):
            block = normed(read, i, j)
            if i == 0:
                NS[j] = block
            ACC[i] += dot(block, Wq[j, 0:C, :])

    def project_all(read, slot, dst):
        rms(read, slot)
        ACC[0] = jnp.zeros((T, Q), F32)

        def step(j, carry):
            ACC[0] += dot(normed(read, slot, j), Wq[j, 0:C, :])
            return carry

        lax.fori_loop(0, 8, step, 0)
        PR[dst] = ACC[0].astype(BF16)

    def head(h):
        return slice(h * HD, (h + 1) * HD)

    def attention(src, mask_slot, probs, t_off):
        def step(h, carry):
            allowed = MASK[mask_slot] > 0.5
            s = dot_nt(PR[src, :, head(h)], PR[src, :, A : A + HD]) * scale
            s = jnp.where(allowed, s, -1e30)
            e = jnp.where(allowed, jnp.exp(s - jnp.max(s, axis=1, keepdims=True)), 0.0)
            p = e / jnp.sum(e, axis=1, keepdims=True)
            if probs:
                PROBS[h] = p
            out = dot(p.astype(BF16), PR[src, :, A + HD : A + 2 * HD])
            if probs:
                ATT_T[head(h), t_off : t_off + T] = out.T.astype(BF16)
            else:
                ATTN[:, head(h)] = out.astype(BF16)
            return carry

        for h in range(HEADS):
            step(h, 0)

    def attention_back(src, dst):
        GK[...] = jnp.zeros_like(GK)
        GV[...] = jnp.zeros_like(GV)

        def step(h, carry):
            d_head = DATT[:, head(h)]
            p = PROBS[h]
            dp = dot_nt(d_head, PR[src, :, A + HD : A + 2 * HD])
            inner = jnp.sum(dp * p, axis=1, keepdims=True)
            ds = (p * (dp - inner) * scale).astype(BF16)
            DP[dst, :, head(h)] = dot(ds, PR[src, :, A : A + HD]).astype(BF16)
            GK[...] += dot_tn(ds, PR[src, :, head(h)])
            GV[...] += dot_tn(p.astype(BF16), d_head)
            return carry

        for h in range(HEADS):
            step(h, 0)
        DP[dst, :, A : A + HD] = GK[...].astype(BF16)
        DP[dst, :, A + HD : A + 2 * HD] = GV[...].astype(BF16)

    def d_att_piece(j):
        DACC[...] += dot_nt(COT[:, cols(j)], Wp[j])

    make_mask(0, 1, 0)
    make_mask(0, 0, 1)
    for j in range(8):
        Gq[j, C : C + PAD, :] = jnp.zeros((PAD, Q), BF16)
    ACC[...] = jnp.zeros_like(ACC)
    DACC[...] = jnp.zeros_like(DACC)
    loads["xs"].wait()
    rms(read_s, 0)
    loads["xf"].wait()
    rms(read_f, 1)
    loads["cot"].wait()
    arrived("seg", SEG.at[1])
    make_mask(1, 1, 2)
    make_mask(1, 0, 3)

    @pl.when(odd == 1)
    def _():
        pl.semaphore_wait(go, 1)
        for copy in first_copies:
            copy.start()

    arrived_part("qZ", 0, Wq.at[oz])
    send_part("cL", 0, Wq.at[oz], Wq.at[oz], left)
    send_part("cR", 0, Wq.at[oz], Wq.at[oz], right)
    send("pZ0", Wp.at[own], Wp.at[own], across)
    arrived("pR", Wp.at[jL])
    send("pRf", Wp.at[jL, pl.ds(0, H2)], Wp.at[jL, pl.ds(0, H2)], right)
    send("pZ1", Wp.at[jL], Wp.at[jL], across)
    arrived("pL", Wp.at[jR])
    send("pLf", Wp.at[jR, pl.ds(H2, H2)], Wp.at[jR, pl.ds(H2, H2)], left)
    send("pZ2", Wp.at[jR], Wp.at[jR], across)
    arrived_part("qZ", 1, Wq.at[oz])
    send_part("cL", 1, Wq.at[oz], Wq.at[oz], left)
    send_part("cR", 1, Wq.at[oz], Wq.at[oz], right)
    send_both("qL", Wq.at[own], Wq.at[own], left)
    arrived_part("qR", 0, Wq.at[jL])
    send_part("eR", 0, Wq.at[jL], Wq.at[jL], right)
    arrived("xe", XE)
    rms(read_e, 2)
    project_piece(own)
    arrived_part("qR", 1, Wq.at[jL])
    send_part("eR", 1, Wq.at[jL], Wq.at[jL], right)
    arrived("pRf", Wp.at[jF, pl.ds(0, H2)])
    arrived("pLf", Wp.at[jF, pl.ds(H2, H2)])
    send("pZ3", Wp.at[jF], Wp.at[jF], across)
    project_piece(oz)
    project_piece(jL)
    arrived_part("cL", 0, Wq.at[ozR])
    send_part("eL", 0, Wq.at[ozR], Wq.at[ozR], left)
    arrived_both("qL", Wq.at[jR])
    project_piece(jR)
    arrived_part("cL", 1, Wq.at[ozR])
    send_part("eL", 1, Wq.at[ozR], Wq.at[ozR], left)

    @pl.when(odd == 0)
    def _():
        pl.semaphore_signal(go, inc=1, device_id=following, device_id_type=MESH)

    d_att_piece(own)
    d_att_piece(jL)
    d_att_piece(jR)
    d_att_piece(jF)
    project_piece(ozR)
    arrived_both("cR", Wq.at[ozL])
    project_piece(ozL)
    arrived("pZ0", Wp.at[oz])
    d_att_piece(oz)
    arrived("pZ1", Wp.at[ozL])
    d_att_piece(ozL)
    arrived("pZ2", Wp.at[ozR])
    d_att_piece(ozR)
    arrived_both("eR", Wq.at[jF])
    project_piece(jF)
    arrived_both("eL", Wq.at[ozF])
    project_piece(ozF)
    PR[0] = ACC[0].astype(BF16)
    PR[1] = ACC[1].astype(BF16)
    PR[2] = ACC[2].astype(BF16)
    attention(0, 0, True, 0)
    arrived("pZ3", Wp.at[ozF])
    d_att_piece(ozF)
    DATT[...] = DACC[...].astype(BF16)

    attention_back(0, 0)

    def scaled_piece(j, total):
        d_normed = dot_nt(DP[0], Wq[j, 0:C, :])
        v = X[0, :, cols(j)].astype(F32)
        GG[j] = jnp.broadcast_to(jnp.sum(d_normed * (v * wide(INV[0])), axis=0, keepdims=True), (8, C))
        scaled = d_normed * gain_row(j)
        DN[j] = scaled
        return total + folded(scaled * v)

    total = lax.fori_loop(0, 8, scaled_piece, jnp.zeros((T, 128), F32))
    inv = INV[0]
    CO[...] = inv * inv * inv * (jnp.sum(total, axis=1, keepdims=True) * (1.0 / D))
    dx_copies = []
    for k in range(4):
        rows = pl.ds(k * (T // 4), T // 4)
        dx_copies.append(remote(f"dh{k}", X.at[0, rows], DH.at[rows], prev))
    started.extend(dx_copies)

    def send_dx():
        for k in range(4):
            rows = slice(k * (T // 4), (k + 1) * (T // 4))

            def dx_piece(j, carry):
                v = X[0, rows, cols(j)].astype(F32)
                d_wide = wide(INV[0, rows, :]) * DN[j, rows, :] - v * wide(CO[rows, :])
                X[0, rows, cols(j)] = (COT[rows, cols(j)].astype(F32) + d_wide).astype(BF16)
                return carry

            lax.fori_loop(0, 8, dx_piece, 0)
            dx_copies[k].start()

    pl.when(odd == 0)(send_dx)

    hidden_copy = remote("hid", X.at[1], HID, prev)
    started.append(hidden_copy)

    def forward_one():
        attention(1, 1, False, 0)

        def out_piece(j, carry):
            X[1, :, cols(j)] = (X[1, :, cols(j)].astype(F32) + dot(ATTN[...], Wp[j])).astype(BF16)
            return carry

        lax.fori_loop(0, 8, out_piece, 0)
        hidden_copy.start()

    attention(2, 2, True, T)
    pl.when(odd == 0)(forward_one)
    loads["sg"].wait()
    loads["sq"].wait()
    loads["sp"].wait()

    for k in range(4):
        arrived(f"dh{k}", DH.at[pl.ds(k * (T // 4), T // 4)])

    DACC[...] = jnp.zeros_like(DACC)

    def d_att_two(j, carry):
        DACC[...] += dot_nt(DH[:, cols(j)], Wp[j])
        return carry

    lax.fori_loop(0, 8, d_att_two, 0)
    DATT[...] = DACC[...].astype(BF16)
    attention_back(2, 1)

    def is_own(j):
        return jnp.where(j == own, 1.0, 0.0)

    def grad_qkv(j):
        d_normed = dot_nt(DP[1], Wq[j, 0:C, :])
        xi = XE[:, cols(j)].astype(F32) * wide(INV[2])
        gg = GG[j][0:1, :] + jnp.sum(d_normed * xi, axis=0, keepdims=True)
        Gq[j, C : C + PAD, 0:C] = (jnp.broadcast_to(gg, (PAD, C)) + is_own(j) * SG[...]).astype(BF16)
        block = (xi * gain_row(j)).astype(BF16)
        terms = dot_tn(NS[j], DP[0]) + dot_tn(block, DP[1])
        Gq[j, 0:C, :] = (terms + is_own(j) * SQ[...]).astype(BF16)

    def grad_proj(j):
        terms = dot(ATT_T[:, 0:T], COT[:, cols(j)]) + dot(ATT_T[:, T : 2 * T], DH[:, cols(j)])
        Gp[j] = (terms + is_own(j) * SP[...]).astype(BF16)

    def each(count, work):
        def step(k, carry):
            work(k)
            return carry

        lax.fori_loop(0, count, step, 0)

    def add_q(j, slots, first=0, last=C + PAD):
        def work(k):
            rows = pl.ds(pl.multiple_of(first + k * QR, 16), QR)
            v = Gq[j, rows, :].astype(F32)
            for s in slots:
                v = v + RQ[s, rows, :].astype(F32)
            Gq[j, rows, :] = v.astype(BF16)

        each((last - first) // QR, work)

    def add_p(j, base, size, parts):
        def work(k):
            off = pl.multiple_of(k * 16, 16)
            v = Gp[j, pl.ds(base + off, 16), :].astype(F32)
            for ref in parts:
                v = v + ref[pl.ds(off, 16), :].astype(F32)
            Gp[j, pl.ds(base + off, 16), :] = v.astype(BF16)

        each(size // 16, work)

    result_copy = remote("res", HID, out_h, following)
    started.append(result_copy)

    def forward_two():
        arrived("hid", HID)
        project_all(read_h, 3, 2)
        attention(2, 3, False, 0)

        def result_piece(j, carry):
            HID[:, cols(j)] = (HID[:, cols(j)].astype(F32) + dot(ATTN[...], Wp[j])).astype(BF16)
            return carry

        lax.fori_loop(0, 8, result_piece, 0)
        result_copy.start()

    grad_qkv(jF)

    @pl.when(odd == 0)
    def _():
        pl.semaphore_wait(turn, 1)

    send_both("m1R", Gq.at[jF], RQ.at[0], right)
    grad_qkv(ozF)
    send_both("m1L", Gq.at[ozF], RQ.at[1], left)
    pl.when(odd == 1)(send_dx)
    each(2, lambda k: grad_qkv(at(z + k, x + 1 + 2 * k)))
    each(4, lambda k: grad_proj(at(z_send, k)))
    for q, off in enumerate((2, 1, 3, 0)):
        send(f"z{q}", Gp.at[at(z_send, x + off)], RPZ.at[q], across)
    for k in range(2):
        arrived_part("m1R", k, RQ.at[0])
        add_q(jR, (0,), *spans[k])
        send_part("m3R", k, Gq.at[jR], RQ.at[4], right)
        arrived_part("m1L", k, RQ.at[1])
        add_q(ozL, (1,), *spans[k])
        send_part("m3L", k, Gq.at[ozL], RQ.at[5], left)
        if k == 0:
            each(2, lambda k: grad_qkv(at(z + 1 + k, x + 1 + 2 * k)))
    for k in range(2):
        send_part("m2R", k, Gq.at[ozR], RQ.at[2], right)
        send_part("m2L", k, Gq.at[jL], RQ.at[3], left)

    @pl.when(odd == 1)
    def _():
        pl.semaphore_signal(turn, inc=1, device_id=prev, device_id_type=MESH)

    pl.when(odd == 1)(forward_two)
    pl.when(odd == 1)(forward_one)
    each(2, lambda k: grad_qkv(at(z + k, x)))
    each(4, lambda k: grad_proj(at(z_keep, k)))
    pl.when(odd == 0)(forward_two)

    kF, kR, kL, kO = (at(z_keep, x + off) for off in (2, 1, 3, 0))
    top, low = pl.ds(0, H2), pl.ds(H2, H2)
    arrived("z0", RPZ.at[0])
    add_p(kF, 0, A, (RPZ.at[0],))
    send("p1R", Gp.at[kF, top], RPX.at[0], right)
    send("p1L", Gp.at[kF, low], RPX.at[1], left)
    arrived("z1", RPZ.at[1])
    add_p(kR, 0, A, (RPZ.at[1],))
    send("p2R", Gp.at[kR, low], RPX.at[2], right)
    arrived("z2", RPZ.at[2])
    add_p(kL, 0, A, (RPZ.at[2],))
    send("p2L", Gp.at[kL, top], RPX.at[3], left)
    j_send, j_keep = at(z_send, x), at(z_keep, x)
    for k in range(2):
        arrived_part("m2R", k, RQ.at[2])
        arrived_part("m2L", k, RQ.at[3])
        arrived_part("m3R", k, RQ.at[4])
        arrived_part("m3L", k, RQ.at[5])
        add_q(j_send, (2 + odd, 5 - odd), *spans[k])
        send_part("mZ", k, Gq.at[j_send], RQ.at[6], across)
    arrived("p1R", RPX.at[0])
    add_p(kR, 0, H2, (RPX.at[0],))
    send("p3R", Gp.at[kR, top], RPX.at[4], right)
    arrived("p1L", RPX.at[1])
    add_p(kL, H2, H2, (RPX.at[1],))
    send("p3L", Gp.at[kL, low], RPX.at[5], left)
    add_q(j_keep, (3 - odd, 4 + odd))
    arrived("z3", RPZ.at[3])
    arrived("p2R", RPX.at[2])
    arrived("p2L", RPX.at[3])
    arrived("p3R", RPX.at[4])
    arrived("p3L", RPX.at[5])
    add_p(kO, 0, H2, (RPZ.at[3, top], RPX.at[4], RPX.at[3]))
    add_p(kO, H2, H2, (RPZ.at[3, low], RPX.at[2], RPX.at[5]))
    send("fp", Gp.at[kO], out_p, following)
    for k in range(2):
        arrived_part("mZ", k, RQ.at[6])
        add_q(j_keep, (6,), *spans[k])
        send_part("fq", k, Gq.at[j_keep], out_q, following)

    arrived("res", out_h)
    arrived("fp", out_p)
    arrived_both("fq", out_q)
    for copy in started:
        copy.wait_send()


def widen(hidden_ref, q_ref, g_ref, p_ref, out_h, out_g, out_q, out_p):
    out_h[...] = hidden_ref[...]
    out_g[...] = g_ref[...].astype(F32)[0:1, : out_g.shape[1]]
    out_q[...] = q_ref[...].astype(F32)
    out_p[...] = p_ref[...].astype(F32)


def body(
    n_blk, x_forward, seg_forward, x_saved, x_earlier, cotangent, seg_backward,
    gain, qkv, proj, sum_gain, sum_qkv, sum_proj,
):
    T, D = x_forward.shape
    C, Q = qkv.shape[1:]
    A = proj.shape[1]
    HD = A // HEADS
    anywhere = pl.BlockSpec(memory_space=pl.ANY)
    V = pltpu.VMEM
    scratch = [
        V((8, C + PAD, Q), BF16), V((8, A, C), BF16), V((8, C + PAD, Q), BF16), V((8, A, C), BF16),
        V((7, C + PAD, Q), BF16), V((4, A, C), BF16), V((6, A // 2, C), BF16),
        V((2, T, D), BF16), V((T, D), BF16), V((T, D), BF16), V((T, D), BF16), V((T, D), BF16),
        V((8, T, C), F32), V((8, T, C), BF16), V((3, T, Q), F32), V((3, T, Q), BF16),
        V((T, A), BF16), V((A, 2 * T), BF16), V((HEADS, T, T), F32), V((2, T, Q), BF16),
        V((T, A), BF16), V((T, A), F32), V((4, T, T), F32), V((T, HD), F32), V((T, HD), F32),
        V((4, T, 128), F32), V((T, 128), F32), V((8, 8, C), F32), V((2, 1, T), jnp.int32),
        V((2, 2, 8, T), F32), V((1, C), BF16), V((1, C), F32), V((C, Q), F32), V((A, C), F32),
        pltpu.SemaphoreType.REGULAR, pltpu.SemaphoreType.REGULAR,
        pltpu.SemaphoreType.DMA((len(MESSAGES),)),
        pltpu.SemaphoreType.DMA((len(MESSAGES),)),
        pltpu.SemaphoreType.DMA((len(LOADS),)),
    ]
    hidden, new_q, new_p = pl.pallas_call(
        functools.partial(kernel, n_blk),
        out_shape=(
            jax.ShapeDtypeStruct((T, D), BF16),
            jax.ShapeDtypeStruct((C + PAD, Q), BF16),
            jax.ShapeDtypeStruct((A, C), BF16),
        ),
        in_specs=[anywhere] * 12,
        out_specs=(anywhere,) * 3,
        scratch_shapes=scratch,
        compiler_params=pltpu.CompilerParams(
            collective_id=0, has_side_effects=True, vmem_limit_bytes=VMEM_LIMIT
        ),
        name="two_steps",
    )(
        x_forward, x_saved, x_earlier, cotangent, seg_forward, seg_backward, qkv[0], gain, proj[0],
        sum_gain, sum_qkv[0], sum_proj[0],
    )
    n = 4
    hidden, new_g, new_q, new_p = pl.pallas_call(
        widen,
        grid=(n,),
        out_shape=(
            jax.ShapeDtypeStruct((T, D), BF16),
            jax.ShapeDtypeStruct((1, C), F32),
            jax.ShapeDtypeStruct((C, Q), F32),
            jax.ShapeDtypeStruct((A, C), F32),
        ),
        in_specs=[
            pl.BlockSpec((T // n, D), lambda i: (i, 0)),
            pl.BlockSpec((C // n, Q), lambda i: (i, 0)),
            pl.BlockSpec((PAD, Q), lambda i: (C // PAD, 0)),
            pl.BlockSpec((A // n, C), lambda i: (i, 0)),
        ],
        out_specs=(
            pl.BlockSpec((T // n, D), lambda i: (i, 0)),
            pl.BlockSpec((1, C), lambda i: (0, 0)),
            pl.BlockSpec((C // n, Q), lambda i: (i, 0)),
            pl.BlockSpec((A // n, C), lambda i: (i, 0)),
        ),
        name="widen",
    )(hidden, new_q, new_q, new_p)
    return hidden, new_g, new_q[None], new_p[None]


def solution(mesh):
    rows, layer = P(("blk", "fsdp"), None), P("blk", "fsdp")
    q_spec, p_spec = P("blk", "fsdp", None), P("blk", None, "fsdp")
    return jax.shard_map(
        functools.partial(body, mesh.shape["blk"]),
        mesh=mesh,
        in_specs=(rows,) * 6 + (layer, q_spec, p_spec) * 2,
        out_specs=(rows, layer, q_spec, p_spec),
        check_vma=False,
    )
```
